32 devices in a mesh: group: 2 (over y), expert: 16 (over z, x, core), tensor: 1.
Axes of the slice: x: 2, y: 2, z: 4, core: 2. Of those that a mesh axis runs over, the one named last changes fastest.
Arguments:
- residual: bfloat16 [2048, 3584], P(('group', 'expert', 'tensor')), parts along dimension 0, may hold values from -6 to 6
- head_partials: bfloat16 [1, 2048, 3584], P('tensor', ('group', 'expert')), parts along dimension 1, may hold values from -6 to 6
- norm_gain: float32 [3584], replicated, may hold values from 0.1 to 1.9
- router_weight: float32 [3584, 16], replicated, as said below
- routes: int32 [2048, 8], P(('group', 'expert', 'tensor')), parts along dimension 0, may hold values from 0 to 15, all different within a row; in each aligned block of 64 rows (0 to 63, 64 to 127, ...) at most 48 rows name the same one
- expert_gate: bfloat16 [16, 3584, 1024], P('expert', None, 'tensor'), may hold values from -0.09375 to 0.09375
- expert_up: bfloat16 [16, 3584, 1024], P('expert', None, 'tensor'), may hold values from -0.09375 to 0.09375
- expert_down: bfloat16 [16, 1024, 3584], P('expert', 'tensor'), may hold values from -0.1875 to 0.1875
Outputs:
- mixed: bfloat16 [2048, 3584], P(('group', 'expert', 'tensor')), parts along dimension 0
The draws below stay inside these ranges and needn't reach their ends.
There are 2 independent parts, one for each index of `group`. The reference program is written for one: setup_inputs(seed, part) draws one part's arguments, and reference() takes and returns one part's arrays. A program takes and returns all parts, laid end to end along the dimension named above; an argument that names none is the same for every part. Nothing has to cross between parts.
Inputs may be any that keep to these rules, and one draw needn't show every extreme that they name: `routes`: each node names 8 different experts. Among the 64 nodes of one device no expert is named by more than 48 nodes, and in some devices' nodes one expert is named by exactly 48. `router_weight`: independent entries, each within 2 / sqrt(3584) of zero.
All inputs are finite; a program needn't handle non-finite values.
Results may differ from the reference program's by a relative error of at most 0.019.
Values may be sent and summed in bfloat16 or wider, within the bound.
A program may use at most 128 MiB of HBM per device.

```python
import math
import jax
import jax.numpy as jnp
import numpy as np
from jax import lax

D = 3584
EXPERT_HIDDEN = 1024
QBLOCK = 128
TOPK = 8
ROWS_DEV = 64
ROWS = 1024
EXPERTS = 16
CAP = 48
N_TENSOR = 1


def draw_router_weight(key, part):
    key = jax.random.fold_in(key, 11)
    spread = 0.5 / math.sqrt(D)
    values = jax.random.truncated_normal(key, -4.0, 4.0, (D, EXPERTS), jnp.float32)
    return (values * spread).astype(jnp.float32)


def shard_levels(own_key, extent, cuts, low, top_value):
    gain = 1.0
    for position, parts in cuts:
        steps = jax.random.uniform(jax.random.fold_in(jax.random.fold_in(own_key, 6), position), (parts,), jnp.float32, low / len(cuts), top_value / len(cuts))
        gain = gain * jnp.repeat(jnp.exp(steps), extent[position] // parts).reshape((-1,) + (1,) * (len(extent) - 1 - position))
    return gain


def routed_block(stream_key, own, number, rows, number_of, top, most, slope):
    order = jax.random.permutation(stream_key, number_of)
    heavy_load, ordinary = shares(number_of, rows * top, most, slope, True), shares(number_of, rows * top, most, slope, False)
    places = jnp.arange(number_of)

    def named(lengths, rotation):
        used = int((lengths > 0).sum())
        fixed = max(1, used // 4)
        passed = fixed + (places - fixed + rotation * (used - fixed)) % max(1, number_of - fixed)
        return jnp.zeros((number_of,), jnp.int32).at[order[jnp.where(places < fixed, places, passed)]].set(jnp.asarray(lengths, jnp.int32))

    lengths = jnp.where(number % 4 == 0, named(heavy_load, number // 4), named(ordinary, number - number // 4 - 1))
    mixed = jax.random.permutation(jax.random.fold_in(own, 3), number_of)
    source_of, receiver = mixed[0:number_of // 2 * 2:2], mixed[1:number_of // 2 * 2:2]
    room = jnp.minimum(lengths[source_of] - 1, most - lengths[receiver]) // 2
    room = jnp.where((source_of == order[0]) | (receiver == order[0]) | (lengths[receiver] == 0), 0, jnp.maximum(room, 0))
    passed = jax.random.randint(jax.random.fold_in(own, 4), (number_of // 2,), 0, 1 << 20) % (room + 1)
    lengths = lengths.at[source_of].add(-passed).at[receiver].add(passed)
    items = jnp.searchsorted(jnp.cumsum(lengths), jnp.arange(rows * top), side="right").astype(jnp.int32)
    grid = items.reshape(top, rows).T
    grid = grid[jax.random.permutation(jax.random.fold_in(own, 1), rows)]
    rotation = jax.random.randint(jax.random.fold_in(own, 2), (rows, 1), 0, top)
    return jnp.take_along_axis(grid, (jnp.arange(top)[None, :] + rotation) % top, axis=1)


def shares(amount, total, most, skew, full):
    loads = [(1 << 20) // math.isqrt(standing ** skew) + 1 for standing in range(1, amount + 1)]
    largest = most if full else min(most, max(-(-total // amount), total * loads[0] // sum(loads)))
    least = 1 if total - largest >= amount - 1 else 0
    holding, rest = [largest] + [least] * (amount - 1), total - largest - least * (amount - 1)
    while rest > 0:
        candidates = [i for i in range(1, amount) if holding[i] < largest] or [i for i in range(1, amount) if holding[i] < most]
        pool, remaining = sum([loads[i] for i in candidates]), rest
        for i in candidates:
            more = min(most - holding[i], max(1, remaining * loads[i] // pool), rest)
            holding[i] = holding[i] + more
            rest = rest - more
    return np.array(holding)


def scatter_about(own_key, dims, scale, most, cuts=(), kind=jnp.bfloat16):
    loudness = shard_levels(own_key, dims, cuts, -0.22, 0.18) if cuts else 1.0
    entries = jax.random.normal(own_key, dims, jnp.float32) * scale * loudness
    return jnp.minimum(jnp.maximum(entries, -most), most).astype(kind)


def setup_inputs(seed: int = 0, part: int = 0) -> dict:
    keys = jax.random.split(jax.random.key(seed), 9)
    own_keys = jax.random.split(jax.random.fold_in(keys[8], part), 9)
    residual = scatter_about(own_keys[0], (ROWS, D), 1.0, 6.0, ((0, 16),))
    head_partials = scatter_about(own_keys[1], (N_TENSOR, ROWS, D), 1.0, 6.0, ((1, 16),))
    norm_gain = jnp.clip(1.0 + 0.18 * jax.random.normal(keys[2], (D,), jnp.float32), 0.1, 1.9)
    router_weight = draw_router_weight(jax.random.fold_in(keys[8], 71), part)
    routes_keys = jax.random.split(jax.random.fold_in(own_keys[4], 1), ROWS // ROWS_DEV)
    routes_turns = jax.random.permutation(jax.random.fold_in(own_keys[4], 3), ROWS // ROWS_DEV)
    routes = jax.vmap(lambda own, number: routed_block(jax.random.fold_in(own_keys[4], 2), own, number, ROWS_DEV, EXPERTS, TOPK, CAP, 2))(routes_keys, routes_turns).reshape((ROWS, TOPK))
    expert_gate = scatter_about(keys[5], (EXPERTS, D, EXPERT_HIDDEN), D ** -0.5, 0.09375, ((0, 16),))
    expert_up = scatter_about(keys[6], (EXPERTS, D, EXPERT_HIDDEN), D ** -0.5, 0.09375, ((0, 16),))
    expert_down = scatter_about(keys[7], (EXPERTS, EXPERT_HIDDEN, D), EXPERT_HIDDEN ** -0.5, 0.1875, ((0, 16),))
    return dict(residual=residual, head_partials=head_partials, norm_gain=norm_gain, router_weight=router_weight, routes=routes, expert_gate=expert_gate, expert_up=expert_up, expert_down=expert_down)


epsilon = 1e-06
scale_limit = 448.0
route_scale = 2.5

def prepare(residual, attention, norm_gain):
    stream = (residual.astype(jnp.float32) + attention).astype(jnp.bfloat16)
    values = stream.astype(jnp.float32)
    normed = values * lax.rsqrt(lax.optimization_barrier(jnp.mean(values * values, axis=-1, keepdims=True)) + epsilon) * norm_gain
    return (stream, normed)

def quantize(normed, block_size):
    row_count = normed.shape[0]
    blocks = normed.reshape(row_count, -1, block_size)
    scales = ((lax.optimization_barrier(jnp.max(jnp.abs(blocks), axis=-1)) + epsilon) / scale_limit).astype(jnp.bfloat16)
    payload = (blocks / scales.astype(jnp.float32)[:, :, None]).astype(jnp.bfloat16)
    return (payload.reshape(row_count, -1), scales)

def dequantize(payload, scales):
    row_count = payload.shape[0]
    block_size = payload.shape[1] // scales.shape[1]
    blocks = payload.astype(jnp.float32).reshape(row_count, scales.shape[1], block_size)
    blocks = blocks * scales.astype(jnp.float32)[:, :, None]
    return blocks.reshape(row_count, -1).astype(jnp.bfloat16)

def route_weights(normed, router_weight, routes):
    logits = jnp.dot(normed, router_weight, precision=lax.Precision.HIGHEST, preferred_element_type=jnp.float32)
    affinity = jax.nn.sigmoid(logits)
    labels = jnp.arange(affinity.shape[1], dtype=jnp.int32)
    picked = lax.optimization_barrier(jnp.sum(jnp.where(routes[:, :, None] == labels[None, None, :], affinity[:, None, :], jnp.float32(0.0)), axis=-1))
    return route_scale * picked / lax.optimization_barrier(jnp.sum(picked, axis=1, keepdims=True))

def expert_apply(inputs, gate_matrix, up_matrix, down_matrix):
    gate_part = jnp.dot(inputs, gate_matrix, preferred_element_type=jnp.float32)
    up_part = jnp.dot(inputs, up_matrix, preferred_element_type=jnp.float32)
    activated = (jax.nn.silu(gate_part) * up_part).astype(jnp.bfloat16)
    portion_width = activated.shape[1] // N_TENSOR
    summed = jnp.zeros((inputs.shape[0], down_matrix.shape[1]), jnp.float32)
    for portion in range(N_TENSOR):
        lower_edge = portion * portion_width
        half_out = jnp.dot(activated[:, lower_edge:lower_edge + portion_width], down_matrix[lower_edge:lower_edge + portion_width], preferred_element_type=jnp.float32).astype(jnp.bfloat16)
        summed = summed + half_out.astype(jnp.float32)
    return summed.astype(jnp.bfloat16)

def reference(residual, head_partials, norm_gain, router_weight, routes, expert_gate, expert_up, expert_down):
    attention = lax.optimization_barrier(jnp.sum(head_partials.astype(jnp.float32), axis=0))
    stream, normed = prepare(residual, attention, norm_gain)
    payload, scales = quantize(normed, QBLOCK)
    weights = route_weights(normed, router_weight, routes)
    inputs = dequantize(payload, scales)
    bound = ROWS // ROWS_DEV * CAP

    def one_expert(expert, running):
        member = routes == expert
        row_weight = lax.optimization_barrier(jnp.sum(jnp.where(member, weights, jnp.float32(0.0)), axis=1))
        in_use = jnp.any(member, axis=1)
        picked_rows = jnp.nonzero(in_use, size=bound, fill_value=0)[0].astype(jnp.int32)
        filled = jnp.arange(bound, dtype=jnp.int32) < jnp.sum(in_use.astype(jnp.int32))
        output = expert_apply(inputs[picked_rows], expert_gate[expert], expert_up[expert], expert_down[expert])
        factor = jnp.where(filled, row_weight[picked_rows], jnp.float32(0.0))
        return running.at[picked_rows].add(output.astype(jnp.float32) * factor[:, None])
    moe_sum = lax.fori_loop(0, EXPERTS, one_expert, jnp.zeros((ROWS, D), jnp.float32))
    return (stream.astype(jnp.float32) + moe_sum).astype(jnp.bfloat16)
```

```python
import jax
import jax.numpy as jnp
from jax import lax
from jax.sharding import PartitionSpec as P

QBLOCK = 128


epsilon = 1e-06
scale_limit = 448.0
route_scale = 2.5


def prepare(residual, attention, norm_gain):
    stream = (residual.astype(jnp.float32) + attention).astype(jnp.bfloat16)
    values = stream.astype(jnp.float32)
    normed = (
        values * lax.rsqrt(jnp.mean(values * values, axis=-1, keepdims=True) + epsilon) * norm_gain
    )
    return (stream, normed)


def quantize(normed, block_size):
    row_count = normed.shape[0]
    blocks = normed.reshape(row_count, -1, block_size)
    scales = ((jnp.max(jnp.abs(blocks), axis=-1) + epsilon) / scale_limit).astype(jnp.bfloat16)
    payload = (blocks / scales.astype(jnp.float32)[:, :, None]).astype(jnp.bfloat16)
    return (payload.reshape(row_count, -1), scales)


def dequantize(payload, scales):
    row_count = payload.shape[0]
    block_size = payload.shape[1] // scales.shape[1]
    blocks = payload.astype(jnp.float32).reshape(row_count, scales.shape[1], block_size)
    blocks = blocks * scales.astype(jnp.float32)[:, :, None]
    return blocks.reshape(row_count, -1).astype(jnp.bfloat16)


def route_weights(normed, router_weight, routes):
    logits = jnp.dot(
        normed, router_weight, precision=lax.Precision.HIGHEST, preferred_element_type=jnp.float32
    )
    affinity = jax.nn.sigmoid(logits)
    labels = jnp.arange(affinity.shape[1], dtype=jnp.int32)
    picked = jnp.sum(
        jnp.where(
            routes[:, :, None] == labels[None, None, :], affinity[:, None, :], jnp.float32(0.0)
        ),
        axis=-1,
    )
    return route_scale * picked / jnp.sum(picked, axis=1, keepdims=True)


def routed(
    residual, head_partials, norm_gain, router_weight, routes, expert_gate, expert_up, expert_down
):
    tensor_count = lax.axis_size("tensor")
    expert_count = lax.axis_size("expert")
    row_count = residual.shape[0]
    top_count = routes.shape[1]
    capacity = max(2, min(row_count, 3 * row_count * top_count // (2 * expert_count)))
    attention = lax.psum_scatter(
        head_partials[0].astype(jnp.float32).astype(jnp.bfloat16),
        "tensor",
        scatter_dimension=0,
        tiled=True,
    ).astype(jnp.float32)
    stream, normed = prepare(residual, attention, norm_gain)
    payload, scales = quantize(normed, QBLOCK)
    weights = route_weights(normed, router_weight, routes)
    pair_count = row_count * top_count
    flat_routes = routes.reshape(pair_count)
    onehot = (flat_routes[:, None] == jnp.arange(expert_count, dtype=jnp.int32)[None, :]).astype(
        jnp.bfloat16
    )
    pair_index = jnp.arange(pair_count, dtype=jnp.int32)
    lower = (pair_index[:, None] > pair_index[None, :]).astype(jnp.bfloat16)
    ahead = jnp.dot(lower, onehot, preferred_element_type=jnp.float32)
    position = jnp.sum(ahead * onehot.astype(jnp.float32), axis=1).astype(jnp.int32)
    slot = flat_routes * capacity + position
    slot_index = jnp.arange(expert_count * capacity, dtype=jnp.int32)
    place = (slot_index[:, None] == slot[None, :]).astype(jnp.bfloat16)
    place_rows = jnp.sum(place.reshape(expert_count * capacity, row_count, top_count), axis=2)
    send_payload = jnp.dot(place_rows, payload, preferred_element_type=jnp.float32).astype(
        jnp.bfloat16
    )
    send_payload = send_payload.reshape(expert_count, capacity, -1)
    send_scales = jnp.dot(place_rows, scales, preferred_element_type=jnp.float32).astype(
        jnp.bfloat16
    )
    send_scales = send_scales.reshape(expert_count, capacity, -1)
    doubled_payload = jnp.repeat(send_payload, tensor_count, axis=0)
    doubled_scales = jnp.repeat(send_scales, tensor_count, axis=0)
    arriving = lax.all_to_all(
        doubled_payload, ("expert", "tensor"), split_axis=0, concat_axis=0, tiled=True
    )
    arriving_scales = lax.all_to_all(
        doubled_scales, ("expert", "tensor"), split_axis=0, concat_axis=0, tiled=True
    )
    sources = arriving.shape[0]
    slots = arriving.shape[1]
    inputs = dequantize(
        arriving.reshape(sources * slots, -1), arriving_scales.reshape(sources * slots, -1)
    )
    gate_part = jnp.dot(inputs, expert_gate[0], preferred_element_type=jnp.float32)
    up_part = jnp.dot(inputs, expert_up[0], preferred_element_type=jnp.float32)
    activated = (jax.nn.silu(gate_part) * up_part).astype(jnp.bfloat16)
    partial_value = jnp.dot(activated, expert_down[0], preferred_element_type=jnp.float32).astype(
        jnp.bfloat16
    )
    partial_value = partial_value.reshape(sources, slots, -1)
    back = lax.all_to_all(
        partial_value, ("expert", "tensor"), split_axis=0, concat_axis=0, tiled=True
    )
    paired = back.reshape(expert_count, tensor_count, back.shape[1], back.shape[2])
    returned = jnp.sum(paired.astype(jnp.float32), axis=1).astype(jnp.bfloat16)
    flat_return = returned.reshape(expert_count * capacity, -1)
    pair_out = jnp.dot(place.T, flat_return, preferred_element_type=jnp.float32)
    moe_sum = jnp.sum(pair_out.reshape(row_count, top_count, -1) * weights[:, :, None], axis=1)
    return (stream.astype(jnp.float32) + moe_sum).astype(jnp.bfloat16)


def dense(
    residual, head_partials, norm_gain, router_weight, routes, expert_gate, expert_up, expert_down
):
    row_count = residual.shape[0]
    stream, normed = prepare(residual, head_partials[0].astype(jnp.float32), norm_gain)
    payload, scales = quantize(normed, QBLOCK)
    weights = route_weights(normed, router_weight, routes)
    labels = jnp.arange(router_weight.shape[1], dtype=jnp.int32)
    spread = jnp.sum(
        jnp.where(routes[:, :, None] == labels[None, None, :], weights[:, :, None], 0.0), axis=1
    )
    rows = lax.all_gather(dequantize(payload, scales), "expert", axis=0, tiled=True)
    spread = lax.all_gather(spread, "expert", axis=0, tiled=True)
    mine = jnp.sum(jnp.where(labels[None, :] == lax.axis_index("expert"), spread, 0.0), axis=1)
    gate_part = jnp.dot(rows, expert_gate[0], preferred_element_type=jnp.float32)
    up_part = jnp.dot(rows, expert_up[0], preferred_element_type=jnp.float32)
    activated = (jax.nn.silu(gate_part) * up_part).astype(jnp.bfloat16)
    part = jnp.dot(activated, expert_down[0], preferred_element_type=jnp.float32)
    part = (part * mine[:, None]).astype(jnp.bfloat16)
    moe_sum = lax.psum_scatter(part, "expert", scatter_dimension=0, tiled=True)
    return (stream.astype(jnp.float32) + moe_sum.astype(jnp.float32)).astype(jnp.bfloat16)


def local(*args):
    expert_count, top_count = lax.axis_size("expert"), args[4].shape[1]
    if lax.axis_size("tensor") == 1 and 2 * top_count >= expert_count:
        return dense(*args)
    return routed(*args)


def solution(mesh):
    return jax.shard_map(
        local,
        mesh=mesh,
        in_specs=(
            P(("group", "expert", "tensor"), None),
            P("tensor", ("group", "expert"), None),
            P(),
            P(),
            P(("group", "expert", "tensor"), None),
            P("expert", None, "tensor"),
            P("expert", None, "tensor"),
            P("expert", "tensor", None),
        ),
        out_specs=P(("group", "expert", "tensor"), None),
        check_vma=False,
    )
```

```python
import jax
import jax.numpy as jnp
from jax import lax
from jax.experimental import pallas as pl
from jax.experimental.pallas import tpu as pltpu
from jax.sharding import PartitionSpec as P

QBLOCK = 128


epsilon = 1e-06
scale_limit = 448.0
route_scale = 2.5


def prepare(residual, attention, norm_gain):
    stream = (residual.astype(jnp.float32) + attention).astype(jnp.bfloat16)
    values = stream.astype(jnp.float32)
    normed = (
        values * lax.rsqrt(jnp.mean(values * values, axis=-1, keepdims=True) + epsilon) * norm_gain
    )
    return (stream, normed)


def quantize(normed, block_size):
    row_count = normed.shape[0]
    blocks = normed.reshape(row_count, -1, block_size)
    scales = ((jnp.max(jnp.abs(blocks), axis=-1) + epsilon) / scale_limit).astype(jnp.bfloat16)
    payload = (blocks / scales.astype(jnp.float32)[:, :, None]).astype(jnp.bfloat16)
    return (payload.reshape(row_count, -1), scales)


def dequantize(payload, scales):
    row_count = payload.shape[0]
    block_size = payload.shape[1] // scales.shape[1]
    blocks = payload.astype(jnp.float32).reshape(row_count, scales.shape[1], block_size)
    blocks = blocks * scales.astype(jnp.float32)[:, :, None]
    return blocks.reshape(row_count, -1).astype(jnp.bfloat16)


def route_weights(normed, router_weight, routes):
    logits = jnp.dot(
        normed, router_weight, precision=lax.Precision.HIGHEST, preferred_element_type=jnp.float32
    )
    affinity = jax.nn.sigmoid(logits)
    labels = jnp.arange(affinity.shape[1], dtype=jnp.int32)
    picked = jnp.sum(
        jnp.where(
            routes[:, :, None] == labels[None, None, :], affinity[:, None, :], jnp.float32(0.0)
        ),
        axis=-1,
    )
    return route_scale * picked / jnp.sum(picked, axis=1, keepdims=True)


def routed(
    residual, head_partials, norm_gain, router_weight, routes, expert_gate, expert_up, expert_down
):
    tensor_count = lax.axis_size("tensor")
    expert_count = lax.axis_size("expert")
    row_count = residual.shape[0]
    top_count = routes.shape[1]
    capacity = max(2, min(row_count, 3 * row_count * top_count // (2 * expert_count)))
    attention = lax.psum_scatter(
        head_partials[0].astype(jnp.float32).astype(jnp.bfloat16),
        "tensor",
        scatter_dimension=0,
        tiled=True,
    ).astype(jnp.float32)
    stream, normed = prepare(residual, attention, norm_gain)
    payload, scales = quantize(normed, QBLOCK)
    weights = route_weights(normed, router_weight, routes)
    pair_count = row_count * top_count
    flat_routes = routes.reshape(pair_count)
    onehot = (flat_routes[:, None] == jnp.arange(expert_count, dtype=jnp.int32)[None, :]).astype(
        jnp.bfloat16
    )
    pair_index = jnp.arange(pair_count, dtype=jnp.int32)
    lower = (pair_index[:, None] > pair_index[None, :]).astype(jnp.bfloat16)
    ahead = jnp.dot(lower, onehot, preferred_element_type=jnp.float32)
    position = jnp.sum(ahead * onehot.astype(jnp.float32), axis=1).astype(jnp.int32)
    slot = flat_routes * capacity + position
    slot_index = jnp.arange(expert_count * capacity, dtype=jnp.int32)
    place = (slot_index[:, None] == slot[None, :]).astype(jnp.bfloat16)
    place_rows = jnp.sum(place.reshape(expert_count * capacity, row_count, top_count), axis=2)
    send_payload = jnp.dot(place_rows, payload, preferred_element_type=jnp.float32).astype(
        jnp.bfloat16
    )
    send_payload = send_payload.reshape(expert_count, capacity, -1)
    send_scales = jnp.dot(place_rows, scales, preferred_element_type=jnp.float32).astype(
        jnp.bfloat16
    )
    send_scales = send_scales.reshape(expert_count, capacity, -1)
    doubled_payload = jnp.repeat(send_payload, tensor_count, axis=0)
    doubled_scales = jnp.repeat(send_scales, tensor_count, axis=0)
    arriving = lax.all_to_all(
        doubled_payload, ("expert", "tensor"), split_axis=0, concat_axis=0, tiled=True
    )
    arriving_scales = lax.all_to_all(
        doubled_scales, ("expert", "tensor"), split_axis=0, concat_axis=0, tiled=True
    )
    sources = arriving.shape[0]
    slots = arriving.shape[1]
    inputs = dequantize(
        arriving.reshape(sources * slots, -1), arriving_scales.reshape(sources * slots, -1)
    )
    gate_part = jnp.dot(inputs, expert_gate[0], preferred_element_type=jnp.float32)
    up_part = jnp.dot(inputs, expert_up[0], preferred_element_type=jnp.float32)
    activated = (jax.nn.silu(gate_part) * up_part).astype(jnp.bfloat16)
    partial_value = jnp.dot(activated, expert_down[0], preferred_element_type=jnp.float32).astype(
        jnp.bfloat16
    )
    partial_value = partial_value.reshape(sources, slots, -1)
    back = lax.all_to_all(
        partial_value, ("expert", "tensor"), split_axis=0, concat_axis=0, tiled=True
    )
    paired = back.reshape(expert_count, tensor_count, back.shape[1], back.shape[2])
    returned = jnp.sum(paired.astype(jnp.float32), axis=1).astype(jnp.bfloat16)
    flat_return = returned.reshape(expert_count * capacity, -1)
    pair_out = jnp.dot(place.T, flat_return, preferred_element_type=jnp.float32)
    moe_sum = jnp.sum(pair_out.reshape(row_count, top_count, -1) * weights[:, :, None], axis=1)
    return (stream.astype(jnp.float32) + moe_sum).astype(jnp.bfloat16)


LAYERS = 4


def pick(table, z):
    value = table[0]
    for i in range(1, LAYERS):
        value = value + (table[i] - table[i - 1]) * ((z + LAYERS - i) // LAYERS)
    return value


def spread_weights(weights, routes, expert_count):
    labels = jnp.arange(expert_count, dtype=jnp.int32)
    return jnp.sum(
        jnp.where(routes[:, :, None] == labels[None, None, :], weights[:, :, None], 0.0), axis=1
    )


def split_three(value):
    first = lax.reduce_precision(value, 8, 7)
    second = lax.reduce_precision(value - first, 8, 7)
    third = value - first - second
    return jnp.concatenate([first, second, third], axis=1).astype(jnp.bfloat16)


def layer_kernel(
    own_ref, stream_ref, gate_hbm, up_hbm, down_hbm, out_ref,
    rows, parts, from_core, from_x, from_z, hidden, gate, up, down,
    send_up, send_dn, send_x, send_core, got_rows,
    back_core, back_x, back_z, got_core, got_x, got_z, weight_sem,
):
    n, width = stream_ref.shape
    full = own_ref.shape[1]
    inner = hidden.shape[1]
    experts = LAYERS * 4
    me = lax.axis_index("expert")
    z, x, c = me // 4, (me // 2) % 2, me % 2
    core_dev = me + 1 - 2 * c
    x_dev = me + 2 - 4 * x
    up_dev, dn_dev = me + 4, me - 4

    def block(layer, xx, cc):
        return layer * 4 + xx * 2 + cc

    def span(b):
        return pl.ds(pl.multiple_of(b * n, n), n)

    barrier = pltpu.get_barrier_semaphore()

    def greet(dev):
        pl.semaphore_signal(
            barrier, inc=1, device_id={"expert": dev}, device_id_type=pl.DeviceIdType.MESH
        )

    greet(core_dev)
    greet(x_dev)
    pl.when(z > 0)(lambda: greet(dn_dev))
    pl.when(z < LAYERS - 1)(lambda: greet(up_dev))

    loads = [
        pltpu.make_async_copy(src.at[0], dst, weight_sem.at[i])
        for i, (src, dst) in enumerate(((gate_hbm, gate), (up_hbm, up), (down_hbm, down)))
    ]
    for load in loads:
        load.start()
    pl.semaphore_wait(barrier, 2 + (z + LAYERS - 1) // LAYERS + (2 * LAYERS - 2 - z) // LAYERS)

    def remote(src, dst, ssem, rsem, dev):
        return pltpu.make_async_remote_copy(
            src_ref=src, dst_ref=dst, send_sem=ssem, recv_sem=rsem,
            device_id={"expert": dev}, device_id_type=pl.DeviceIdType.MESH,
        )

    def row_copy(b, sems, dev, src=None):
        return remote(
            rows.at[span(b)] if src is None else src,
            rows.at[span(b)], sems.at[b], got_rows.at[b], dev,
        )

    def arrived(b):
        row_copy(b, send_core, core_dev).wait_recv()

    row_copy(me, send_x, x_dev, own_ref).start()
    pl.when(z > 0)(lambda: row_copy(me, send_dn, dn_dev, own_ref).start())
    pl.when(z < LAYERS - 1)(lambda: row_copy(me, send_up, up_dev, own_ref).start())
    row_copy(me, send_core, core_dev, own_ref).start()
    rows[span(me), :] = own_ref[...]

    def from_line(layer, sems, onward, dev):
        b = block(layer, x, c)
        arrived(b)
        pl.when(onward)(lambda: row_copy(b, sems, dev).start())
        row_copy(b, send_x, x_dev).start()
        row_copy(b, send_core, core_dev).start()

    def line_step(s):
        pl.when(z >= s)(lambda: from_line(z - s, send_up, z < LAYERS - 1, up_dev))
        pl.when(z + s < LAYERS)(lambda: from_line(z + s, send_dn, z > 0, dn_dev))

    def rest_of(layer):
        b = block(layer, 1 - x, c)
        arrived(b)
        row_copy(b, send_core, core_dev).start()
        arrived(block(layer, 0, 1 - c))
        arrived(block(layer, 1, 1 - c))

    def layer_span(layer):
        return pl.ds(pl.multiple_of(layer * 4 * n, 4 * n), 4 * n)

    def compute(layer, first):
        if first:
            loads[0].wait()
            loads[1].wait()
        where = layer_span(layer)

        @pl.loop(0, inner // 256)
        def _(i):
            cols = pl.ds(pl.multiple_of(i * 256, 256), 256)
            inputs = rows[where, :width]
            g = jnp.dot(inputs, gate[:, cols], preferred_element_type=jnp.float32)
            u = jnp.dot(inputs, up[:, cols], preferred_element_type=jnp.float32)
            hidden[:, cols] = (g / (1.0 + jnp.exp(-g)) * u).astype(jnp.bfloat16)

        if first:
            loads[2].wait()
        lane = lax.broadcasted_iota(jnp.int32, (4 * n, full - width), 1)
        mine = (lane == me) | (lane == me + experts) | (lane == me + 2 * experts)
        factor = jnp.sum(
            jnp.where(mine, rows[where, width:].astype(jnp.float32), 0.0), axis=1, keepdims=True
        )

        @pl.loop(0, width // 512)
        def _(i):
            cols = pl.ds(pl.multiple_of(i * 512, 512), 512)
            o = jnp.dot(hidden[...], down[:, cols], preferred_element_type=jnp.float32)
            parts[where, cols] = (o * factor).astype(jnp.bfloat16)

        for xx in range(2):
            core_back(layer, xx, 1 - c).start()

    def core_back(layer, xx, cc):
        slot = layer * 2 + xx
        return remote(
            parts.at[span(block(layer, xx, cc))], from_core.at[slot],
            back_core.at[slot], got_core.at[slot], core_dev,
        )

    def x_back(layer):
        return remote(
            parts.at[span(block(layer, 1 - x, c))], from_x.at[layer],
            back_x.at[layer], got_x.at[layer], x_dev,
        )

    def z_back(layer, slot, dev):
        return remote(
            parts.at[span(block(layer, x, c))], from_z.at[slot],
            back_z.at[layer], got_z.at[slot], dev,
        )

    def add_up(dst, dst_rows, terms):
        @pl.loop(0, width // 512)
        def _(i):
            cols = pl.ds(pl.multiple_of(i * 512, 512), 512)
            total = None
            for ref, where in terms:
                term = ref[where, cols].astype(jnp.float32)
                total = term if total is None else total + term
            dst[dst_rows, cols] = total.astype(jnp.bfloat16)

    whole = slice(None)

    def ret_x(layer):
        core_back(layer, 1 - x, c).wait_recv()
        b = span(block(layer, 1 - x, c))
        add_up(parts, b, [(parts, b), (from_core.at[layer * 2 + 1 - x], whole)])
        x_back(layer).start()

    def ret_z(layer):
        core_back(layer, x, c).wait_recv()
        x_back(layer).wait_recv()
        b = span(block(layer, x, c))
        terms = [
            (parts, b), (from_core.at[layer * 2 + x], whole), (from_x.at[layer], whole),
        ]
        carries = ((layer > z) & (z > 0)) | ((layer < z) & (z < LAYERS - 1))

        @pl.when(carries)
        def _():
            z_back(layer, layer, up_dev).wait_recv()
            add_up(parts, b, terms + [(from_z.at[layer], whole)])

        @pl.when(jnp.logical_not(carries))
        def _():
            add_up(parts, b, terms)

        @pl.when(layer > z)
        def _():
            z_back(layer, layer, up_dev).start()

        @pl.when((layer < z) & (layer < z - 1))
        def _():
            z_back(layer, layer, dn_dev).start()

        @pl.when((layer < z) & (layer == z - 1))
        def _():
            z_back(layer, LAYERS, dn_dev).start()

    order = [
        z,
        pick((1, 2, 1, 2), z),
        pick((2, 0, 3, 1), z),
        pick((3, 3, 0, 0), z),
    ]
    back_order = [order[1], pick((2, 3, 0, 1), z), pick((3, 0, 3, 0), z)]

    line_step(1)
    rest_of(order[0])
    compute(order[0], True)
    line_step(2)
    rest_of(order[1])
    compute(order[1], False)
    ret_x(order[0])
    line_step(3)
    rest_of(order[2])
    compute(order[2], False)
    ret_x(order[1])
    rest_of(order[3])
    compute(order[3], False)
    ret_x(order[2])
    ret_x(order[3])
    for layer in back_order:
        ret_z(layer)

    core_back(z, x, c).wait_recv()
    x_back(z).wait_recv()
    b = span(me)
    terms = [
        (stream_ref, whole), (parts, b), (from_core.at[z * 2 + x], whole), (from_x.at[z], whole),
    ]
    below, above = (from_z.at[z], whole), (from_z.at[LAYERS], whole)

    @pl.when(z > 0)
    def _():
        z_back(z, z, up_dev).wait_recv()

    @pl.when(z < LAYERS - 1)
    def _():
        z_back(z, LAYERS, up_dev).wait_recv()

    @pl.when(z == 0)
    def _():
        add_up(out_ref, whole, terms + [above])

    @pl.when(z == LAYERS - 1)
    def _():
        add_up(out_ref, whole, terms + [below])

    @pl.when((z > 0) & (z < LAYERS - 1))
    def _():
        add_up(out_ref, whole, terms + [below, above])

    for layer in range(LAYERS):
        mine = block(layer, x, c)
        row_copy(mine, send_x, x_dev).wait_send()
        row_copy(mine, send_core, core_dev).wait_send()
        row_copy(block(layer, 1 - x, c), send_core, core_dev).wait_send()

        @pl.when((layer <= z) & (z < LAYERS - 1))
        def _():
            row_copy(mine, send_up, up_dev).wait_send()

        @pl.when((layer >= z) & (z > 0))
        def _():
            row_copy(mine, send_dn, dn_dev).wait_send()

        for xx in range(2):
            core_back(layer, xx, 1 - c).wait_send()
        x_back(layer).wait_send()

        @pl.when(z != layer)
        def _():
            z_back(layer, layer, up_dev).wait_send()


def expert_layer(own, stream, gate, up, down):
    n, width = stream.shape
    full = own.shape[1]
    inner = gate.shape[2]
    total = 4 * LAYERS
    dma = pltpu.SemaphoreType.DMA
    bf16 = jnp.bfloat16
    return pl.pallas_call(
        layer_kernel,
        out_shape=jax.ShapeDtypeStruct((n, width), bf16),
        in_specs=[pl.BlockSpec(memory_space=pltpu.VMEM)] * 2
        + [pl.BlockSpec(memory_space=pl.ANY)] * 3,
        out_specs=pl.BlockSpec(memory_space=pltpu.VMEM),
        scratch_shapes=[
            pltpu.VMEM((total * n, full), bf16),
            pltpu.VMEM((total * n, width), bf16),
            pltpu.VMEM((2 * LAYERS, n, width), bf16),
            pltpu.VMEM((LAYERS, n, width), bf16),
            pltpu.VMEM((LAYERS + 1, n, width), bf16),
            pltpu.VMEM((4 * n, inner), bf16),
            pltpu.VMEM((width, inner), bf16),
            pltpu.VMEM((width, inner), bf16),
            pltpu.VMEM((inner, width), bf16),
            dma((total,)), dma((total,)), dma((total,)), dma((total,)), dma((total,)),
            dma((2 * LAYERS,)), dma((LAYERS,)), dma((LAYERS,)),
            dma((2 * LAYERS,)), dma((LAYERS,)), dma((LAYERS + 1,)),
            dma((3,)),
        ],
        compiler_params=pltpu.CompilerParams(
            collective_id=0, has_side_effects=True, vmem_limit_bytes=60 * 1024 * 1024
        ),
    )(own, stream, gate, up, down)


def dense(
    residual, head_partials, norm_gain, router_weight, routes, expert_gate, expert_up, expert_down
):
    expert_count = router_weight.shape[1]
    stream, normed = prepare(residual, head_partials[0].astype(jnp.float32), norm_gain)
    payload, scales = quantize(normed, QBLOCK)
    weights = route_weights(normed, router_weight, routes)
    spread = split_three(spread_weights(weights, routes, expert_count))
    spread = jnp.pad(spread, ((0, 0), (0, 128 - spread.shape[1])))
    own = jnp.concatenate([dequantize(payload, scales), spread], axis=1)
    return expert_layer(own, stream, expert_gate, expert_up, expert_down)


def local(*args):
    if lax.axis_size("tensor") == 1 and lax.axis_size("expert") == 4 * LAYERS:
        return dense(*args)
    return routed(*args)


def solution(mesh):
    return jax.shard_map(
        local,
        mesh=mesh,
        in_specs=(
            P(("group", "expert", "tensor"), None),
            P("tensor", ("group", "expert"), None),
            P(),
            P(),
            P(("group", "expert", "tensor"), None),
            P("expert", None, "tensor"),
            P("expert", None, "tensor"),
            P("expert", "tensor", None),
        ),
        out_specs=P(("group", "expert", "tensor"), None),
        check_vma=False,
    )
```

```python
import jax
import jax.numpy as jnp
from jax import lax
from jax.experimental import pallas as pl
from jax.experimental.pallas import tpu as pltpu
from jax.sharding import PartitionSpec as P

QBLOCK = 128


epsilon = 1e-06
scale_limit = 448.0
route_scale = 2.5


def prepare(residual, attention, norm_gain):
    stream = (residual.astype(jnp.float32) + attention).astype(jnp.bfloat16)
    values = stream.astype(jnp.float32)
    normed = (
        values * lax.rsqrt(jnp.mean(values * values, axis=-1, keepdims=True) + epsilon) * norm_gain
    )
    return (stream, normed)


def quantize(normed, block_size):
    row_count = normed.shape[0]
    blocks = normed.reshape(row_count, -1, block_size)
    scales = ((jnp.max(jnp.abs(blocks), axis=-1) + epsilon) / scale_limit).astype(jnp.bfloat16)
    payload = (blocks / scales.astype(jnp.float32)[:, :, None]).astype(jnp.bfloat16)
    return (payload.reshape(row_count, -1), scales)


def dequantize(payload, scales):
    row_count = payload.shape[0]
    block_size = payload.shape[1] // scales.shape[1]
    blocks = payload.astype(jnp.float32).reshape(row_count, scales.shape[1], block_size)
    blocks = blocks * scales.astype(jnp.float32)[:, :, None]
    return blocks.reshape(row_count, -1).astype(jnp.bfloat16)


def route_weights(normed, router_weight, routes):
    logits = jnp.dot(
        normed, router_weight, precision=lax.Precision.HIGHEST, preferred_element_type=jnp.float32
    )
    affinity = jax.nn.sigmoid(logits)
    labels = jnp.arange(affinity.shape[1], dtype=jnp.int32)
    picked = jnp.sum(
        jnp.where(
            routes[:, :, None] == labels[None, None, :], affinity[:, None, :], jnp.float32(0.0)
        ),
        axis=-1,
    )
    return route_scale * picked / jnp.sum(picked, axis=1, keepdims=True)


def routed(
    residual, head_partials, norm_gain, router_weight, routes, expert_gate, expert_up, expert_down
):
    tensor_count = lax.axis_size("tensor")
    expert_count = lax.axis_size("expert")
    row_count = residual.shape[0]
    top_count = routes.shape[1]
    capacity = max(2, min(row_count, 3 * row_count * top_count // (2 * expert_count)))
    attention = lax.psum_scatter(
        head_partials[0].astype(jnp.float32).astype(jnp.bfloat16),
        "tensor",
        scatter_dimension=0,
        tiled=True,
    ).astype(jnp.float32)
    stream, normed = prepare(residual, attention, norm_gain)
    payload, scales = quantize(normed, QBLOCK)
    weights = route_weights(normed, router_weight, routes)
    pair_count = row_count * top_count
    flat_routes = routes.reshape(pair_count)
    onehot = (flat_routes[:, None] == jnp.arange(expert_count, dtype=jnp.int32)[None, :]).astype(
        jnp.bfloat16
    )
    pair_index = jnp.arange(pair_count, dtype=jnp.int32)
    lower = (pair_index[:, None] > pair_index[None, :]).astype(jnp.bfloat16)
    ahead = jnp.dot(lower, onehot, preferred_element_type=jnp.float32)
    position = jnp.sum(ahead * onehot.astype(jnp.float32), axis=1).astype(jnp.int32)
    slot = flat_routes * capacity + position
    slot_index = jnp.arange(expert_count * capacity, dtype=jnp.int32)
    place = (slot_index[:, None] == slot[None, :]).astype(jnp.bfloat16)
    place_rows = jnp.sum(place.reshape(expert_count * capacity, row_count, top_count), axis=2)
    send_payload = jnp.dot(place_rows, payload, preferred_element_type=jnp.float32).astype(
        jnp.bfloat16
    )
    send_payload = send_payload.reshape(expert_count, capacity, -1)
    send_scales = jnp.dot(place_rows, scales, preferred_element_type=jnp.float32).astype(
        jnp.bfloat16
    )
    send_scales = send_scales.reshape(expert_count, capacity, -1)
    doubled_payload = jnp.repeat(send_payload, tensor_count, axis=0)
    doubled_scales = jnp.repeat(send_scales, tensor_count, axis=0)
    arriving = lax.all_to_all(
        doubled_payload, ("expert", "tensor"), split_axis=0, concat_axis=0, tiled=True
    )
    arriving_scales = lax.all_to_all(
        doubled_scales, ("expert", "tensor"), split_axis=0, concat_axis=0, tiled=True
    )
    sources = arriving.shape[0]
    slots = arriving.shape[1]
    inputs = dequantize(
        arriving.reshape(sources * slots, -1), arriving_scales.reshape(sources * slots, -1)
    )
    gate_part = jnp.dot(inputs, expert_gate[0], preferred_element_type=jnp.float32)
    up_part = jnp.dot(inputs, expert_up[0], preferred_element_type=jnp.float32)
    activated = (jax.nn.silu(gate_part) * up_part).astype(jnp.bfloat16)
    partial_value = jnp.dot(activated, expert_down[0], preferred_element_type=jnp.float32).astype(
        jnp.bfloat16
    )
    partial_value = partial_value.reshape(sources, slots, -1)
    back = lax.all_to_all(
        partial_value, ("expert", "tensor"), split_axis=0, concat_axis=0, tiled=True
    )
    paired = back.reshape(expert_count, tensor_count, back.shape[1], back.shape[2])
    returned = jnp.sum(paired.astype(jnp.float32), axis=1).astype(jnp.bfloat16)
    flat_return = returned.reshape(expert_count * capacity, -1)
    pair_out = jnp.dot(place.T, flat_return, preferred_element_type=jnp.float32)
    moe_sum = jnp.sum(pair_out.reshape(row_count, top_count, -1) * weights[:, :, None], axis=1)
    return (stream.astype(jnp.float32) + moe_sum).astype(jnp.bfloat16)


LAYERS = 4


def pick(table, z):
    value = table[0]
    for i in range(1, LAYERS):
        value = value + (table[i] - table[i - 1]) * ((z + LAYERS - i) // LAYERS)
    return value


def spread_weights(weights, routes, expert_count):
    labels = jnp.arange(expert_count, dtype=jnp.int32)
    return jnp.sum(
        jnp.where(routes[:, :, None] == labels[None, None, :], weights[:, :, None], 0.0), axis=1
    )


def split_three(value):
    first = lax.reduce_precision(value, 8, 7)
    second = lax.reduce_precision(value - first, 8, 7)
    third = value - first - second
    return jnp.concatenate([first, second, third], axis=1).astype(jnp.bfloat16)


def layer_kernel(
    own_ref, stream_ref, gate_hbm, up_hbm, down_hbm, out_ref,
    rows, parts, from_core, from_x, from_z, hidden, gate, up, down,
    send_up, send_dn, send_x, send_core, got_rows,
    back_core, back_x, back_z, got_core, got_x, got_z, weight_sem,
):
    n, width = stream_ref.shape
    full = own_ref.shape[1]
    inner = hidden.shape[1]
    experts = LAYERS * 4
    me = lax.axis_index("expert")
    z, x, c = me // 4, (me // 2) % 2, me % 2
    core_dev = me + 1 - 2 * c
    x_dev = me + 2 - 4 * x
    up_dev, dn_dev = me + 4, me - 4

    def block(layer, xx, cc):
        return layer * 4 + xx * 2 + cc

    def span(b):
        return pl.ds(pl.multiple_of(b * n, n), n)

    barrier = pltpu.get_barrier_semaphore()

    def greet(dev):
        pl.semaphore_signal(
            barrier, inc=1, device_id={"expert": dev}, device_id_type=pl.DeviceIdType.MESH
        )

    greet(core_dev)
    greet(x_dev)
    pl.when(z > 0)(lambda: greet(dn_dev))
    pl.when(z < LAYERS - 1)(lambda: greet(up_dev))

    loads = [
        pltpu.make_async_copy(src.at[0], dst, weight_sem.at[i])
        for i, (src, dst) in enumerate(((gate_hbm, gate), (up_hbm, up), (down_hbm, down)))
    ]
    for load in loads:
        load.start()
    pl.semaphore_wait(barrier, 2 + (z + LAYERS - 1) // LAYERS + (2 * LAYERS - 2 - z) // LAYERS)

    def remote(src, dst, ssem, rsem, dev):
        return pltpu.make_async_remote_copy(
            src_ref=src, dst_ref=dst, send_sem=ssem, recv_sem=rsem,
            device_id={"expert": dev}, device_id_type=pl.DeviceIdType.MESH,
        )

    def row_copy(b, sems, dev, src=None):
        return remote(
            rows.at[span(b)] if src is None else src,
            rows.at[span(b)], sems.at[b], got_rows.at[b], dev,
        )

    def arrived(b):
        row_copy(b, send_core, core_dev).wait_recv()

    row_copy(me, send_x, x_dev, own_ref).start()
    pl.when(z > 0)(lambda: row_copy(me, send_dn, dn_dev, own_ref).start())
    pl.when(z < LAYERS - 1)(lambda: row_copy(me, send_up, up_dev, own_ref).start())
    row_copy(me, send_core, core_dev, own_ref).start()
    rows[span(me), :] = own_ref[...]

    def from_line(layer, sems, onward, dev):
        b = block(layer, x, c)
        arrived(b)
        pl.when(onward)(lambda: row_copy(b, sems, dev).start())
        row_copy(b, send_x, x_dev).start()
        row_copy(b, send_core, core_dev).start()

    def line_step(s):
        pl.when(z >= s)(lambda: from_line(z - s, send_up, z < LAYERS - 1, up_dev))
        pl.when(z + s < LAYERS)(lambda: from_line(z + s, send_dn, z > 0, dn_dev))

    def rest_of(layer):
        b = block(layer, 1 - x, c)
        arrived(b)
        row_copy(b, send_core, core_dev).start()
        arrived(block(layer, 0, 1 - c))
        arrived(block(layer, 1, 1 - c))

    def layer_span(layer):
        return pl.ds(pl.multiple_of(layer * 4 * n, 4 * n), 4 * n)

    half = (width // 512 + 1) // 2 * 512
    chunks = ((0, half), (half, width - half))

    def part(h):
        return pl.ds(chunks[h][0], chunks[h][1])

    def gate_up(layer):
        where = layer_span(layer)

        @pl.loop(0, inner // 256)
        def _(i):
            cols = pl.ds(pl.multiple_of(i * 256, 256), 256)
            inputs = rows[where, :width]
            g = jnp.dot(inputs, gate[:, cols], preferred_element_type=jnp.float32)
            u = jnp.dot(inputs, up[:, cols], preferred_element_type=jnp.float32)
            hidden[:, cols] = (g / (1.0 + jnp.exp(-g)) * u).astype(jnp.bfloat16)

    def down_back(layer):
        where = layer_span(layer)
        lane = lax.broadcasted_iota(jnp.int32, (4 * n, full - width), 1)
        mine = (lane == me) | (lane == me + experts) | (lane == me + 2 * experts)
        factor = jnp.sum(
            jnp.where(mine, rows[where, width:].astype(jnp.float32), 0.0), axis=1, keepdims=True
        )
        for h in range(2):

            @pl.loop(chunks[h][0] // 512, sum(chunks[h]) // 512)
            def _(i):
                cols = pl.ds(pl.multiple_of(i * 512, 512), 512)
                o = jnp.dot(hidden[...], down[:, cols], preferred_element_type=jnp.float32)
                parts[where, cols] = (o * factor).astype(jnp.bfloat16)

            for xx in (1 - x, x):
                core_back(layer, xx, 1 - c, h).start()

    def core_back(layer, xx, cc, h):
        slot = layer * 2 + xx
        return remote(
            parts.at[span(block(layer, xx, cc)), part(h)], from_core.at[slot, :, part(h)],
            back_core.at[slot, h], got_core.at[slot, h], core_dev,
        )

    def x_back(layer, h):
        return remote(
            parts.at[span(block(layer, 1 - x, c)), part(h)], from_x.at[layer, :, part(h)],
            back_x.at[layer, h], got_x.at[layer, h], x_dev,
        )

    def z_back(layer, slot, dev, h):
        return remote(
            parts.at[span(block(layer, x, c)), part(h)], from_z.at[slot, :, part(h)],
            back_z.at[layer, h], got_z.at[slot, h], dev,
        )

    def add_up(dst, dst_rows, terms, h):
        @pl.loop(chunks[h][0] // 512, sum(chunks[h]) // 512)
        def _(i):
            cols = pl.ds(pl.multiple_of(i * 512, 512), 512)
            total = None
            for ref, where in terms:
                term = ref[where, cols].astype(jnp.float32)
                total = term if total is None else total + term
            dst[dst_rows, cols] = total.astype(jnp.bfloat16)

    whole = slice(None)

    def ret_x(layer):
        b = span(block(layer, 1 - x, c))
        for h in range(2):
            core_back(layer, 1 - x, c, h).wait_recv()
            add_up(parts, b, [(parts, b), (from_core.at[layer * 2 + 1 - x], whole)], h)
            x_back(layer, h).start()

    def ret_z(layer):
        b = span(block(layer, x, c))
        terms = [
            (parts, b), (from_core.at[layer * 2 + x], whole), (from_x.at[layer], whole),
        ]
        carries = ((layer > z) & (z > 0)) | ((layer < z) & (z < LAYERS - 1))
        for h in range(2):
            core_back(layer, x, c, h).wait_recv()
            x_back(layer, h).wait_recv()

            @pl.when(carries)
            def _():
                z_back(layer, layer, up_dev, h).wait_recv()
                add_up(parts, b, terms + [(from_z.at[layer], whole)], h)

            @pl.when(jnp.logical_not(carries))
            def _():
                add_up(parts, b, terms, h)

            @pl.when(layer > z)
            def _():
                z_back(layer, layer, up_dev, h).start()

            @pl.when((layer < z) & (layer < z - 1))
            def _():
                z_back(layer, layer, dn_dev, h).start()

            @pl.when((layer < z) & (layer == z - 1))
            def _():
                z_back(layer, LAYERS, dn_dev, h).start()

    order = [
        z,
        pick((1, 2, 1, 2), z),
        pick((2, 0, 3, 1), z),
        pick((3, 3, 0, 0), z),
    ]
    back_order = [order[1], pick((2, 3, 0, 1), z), pick((3, 0, 3, 0), z)]
    ends = (z == 0) | (z == LAYERS - 1)

    line_step(1)
    rest_of(order[0])
    loads[0].wait()
    loads[1].wait()
    gate_up(order[0])
    loads[2].wait()
    down_back(order[0])
    line_step(2)
    rest_of(order[1])
    gate_up(order[1])
    down_back(order[1])
    line_step(3)
    rest_of(order[2])
    gate_up(order[2])
    ret_x(order[1])
    down_back(order[2])
    rest_of(order[3])
    gate_up(order[3])
    ret_x(order[2])
    pl.when(ends)(lambda: ret_z(order[1]))
    down_back(order[3])
    ret_x(order[3])
    pl.when(ends)(lambda: ret_z(order[2]))
    ret_x(order[0])
    pl.when(ends)(lambda: ret_z(order[3]))

    @pl.when(jnp.logical_not(ends))
    def _():
        for layer in back_order:
            ret_z(layer)

    b = span(me)
    terms = [
        (stream_ref, whole), (parts, b), (from_core.at[z * 2 + x], whole), (from_x.at[z], whole),
    ]
    below, above = (from_z.at[z], whole), (from_z.at[LAYERS], whole)
    for h in range(2):
        core_back(z, x, c, h).wait_recv()
        x_back(z, h).wait_recv()

        @pl.when(z > 0)
        def _():
            z_back(z, z, up_dev, h).wait_recv()

        @pl.when(z < LAYERS - 1)
        def _():
            z_back(z, LAYERS, up_dev, h).wait_recv()

        @pl.when(z == 0)
        def _():
            add_up(out_ref, whole, terms + [above], h)

        @pl.when(z == LAYERS - 1)
        def _():
            add_up(out_ref, whole, terms + [below], h)

        @pl.when((z > 0) & (z < LAYERS - 1))
        def _():
            add_up(out_ref, whole, terms + [below, above], h)

    for layer in range(LAYERS):
        mine = block(layer, x, c)
        row_copy(mine, send_x, x_dev).wait_send()
        row_copy(mine, send_core, core_dev).wait_send()
        row_copy(block(layer, 1 - x, c), send_core, core_dev).wait_send()

        @pl.when((layer <= z) & (z < LAYERS - 1))
        def _():
            row_copy(mine, send_up, up_dev).wait_send()

        @pl.when((layer >= z) & (z > 0))
        def _():
            row_copy(mine, send_dn, dn_dev).wait_send()

        for h in range(2):
            for xx in range(2):
                core_back(layer, xx, 1 - c, h).wait_send()
            x_back(layer, h).wait_send()

            @pl.when(z != layer)
            def _():
                z_back(layer, layer, up_dev, h).wait_send()


def expert_layer(own, stream, gate, up, down):
    n, width = stream.shape
    full = own.shape[1]
    inner = gate.shape[2]
    total = 4 * LAYERS
    dma = pltpu.SemaphoreType.DMA
    bf16 = jnp.bfloat16
    return pl.pallas_call(
        layer_kernel,
        out_shape=jax.ShapeDtypeStruct((n, width), bf16),
        in_specs=[pl.BlockSpec(memory_space=pltpu.VMEM)] * 2
        + [pl.BlockSpec(memory_space=pl.ANY)] * 3,
        out_specs=pl.BlockSpec(memory_space=pltpu.VMEM),
        scratch_shapes=[
            pltpu.VMEM((total * n, full), bf16),
            pltpu.VMEM((total * n, width), bf16),
            pltpu.VMEM((2 * LAYERS, n, width), bf16),
            pltpu.VMEM((LAYERS, n, width), bf16),
            pltpu.VMEM((LAYERS + 1, n, width), bf16),
            pltpu.VMEM((4 * n, inner), bf16),
            pltpu.VMEM((width, inner), bf16),
            pltpu.VMEM((width, inner), bf16),
            pltpu.VMEM((inner, width), bf16),
            dma((total,)), dma((total,)), dma((total,)), dma((total,)), dma((total,)),
            dma((2 * LAYERS, 2)), dma((LAYERS, 2)), dma((LAYERS, 2)),
            dma((2 * LAYERS, 2)), dma((LAYERS, 2)), dma((LAYERS + 1, 2)),
            dma((3,)),
        ],
        compiler_params=pltpu.CompilerParams(
            collective_id=0, has_side_effects=True, vmem_limit_bytes=60 * 1024 * 1024
        ),
    )(own, stream, gate, up, down)


def dense(
    residual, head_partials, norm_gain, router_weight, routes, expert_gate, expert_up, expert_down
):
    expert_count = router_weight.shape[1]
    stream, normed = prepare(residual, head_partials[0].astype(jnp.float32), norm_gain)
    payload, scales = quantize(normed, QBLOCK)
    weights = route_weights(normed, router_weight, routes)
    spread = split_three(spread_weights(weights, routes, expert_count))
    spread = jnp.pad(spread, ((0, 0), (0, 128 - spread.shape[1])))
    own = jnp.concatenate([dequantize(payload, scales), spread], axis=1)
    return expert_layer(own, stream, expert_gate, expert_up, expert_down)


def local(*args):
    if lax.axis_size("tensor") == 1 and lax.axis_size("expert") == 4 * LAYERS:
        return dense(*args)
    return routed(*args)


def solution(mesh):
    return jax.shard_map(
        local,
        mesh=mesh,
        in_specs=(
            P(("group", "expert", "tensor"), None),
            P("tensor", ("group", "expert"), None),
            P(),
            P(),
            P(("group", "expert", "tensor"), None),
            P("expert", None, "tensor"),
            P("expert", None, "tensor"),
            P("expert", "tensor", None),
        ),
        out_specs=P(("group", "expert", "tensor"), None),
        check_vma=False,
    )
```

```python
import jax
import jax.numpy as jnp
from jax import lax
from jax.experimental import pallas as pl
from jax.experimental.pallas import tpu as pltpu
from jax.sharding import PartitionSpec as P

QBLOCK = 128


epsilon = 1e-06
scale_limit = 448.0
route_scale = 2.5


def prepare(residual, attention, norm_gain):
    stream = (residual.astype(jnp.float32) + attention).astype(jnp.bfloat16)
    values = stream.astype(jnp.float32)
    normed = (
        values * lax.rsqrt(jnp.mean(values * values, axis=-1, keepdims=True) + epsilon) * norm_gain
    )
    return (stream, normed)


def quantize(normed, block_size):
    row_count = normed.shape[0]
    blocks = normed.reshape(row_count, -1, block_size)
    scales = ((jnp.max(jnp.abs(blocks), axis=-1) + epsilon) / scale_limit).astype(jnp.bfloat16)
    payload = (blocks / scales.astype(jnp.float32)[:, :, None]).astype(jnp.bfloat16)
    return (payload.reshape(row_count, -1), scales)


def dequantize(payload, scales):
    row_count = payload.shape[0]
    block_size = payload.shape[1] // scales.shape[1]
    blocks = payload.astype(jnp.float32).reshape(row_count, scales.shape[1], block_size)
    blocks = blocks * scales.astype(jnp.float32)[:, :, None]
    return blocks.reshape(row_count, -1).astype(jnp.bfloat16)


def route_weights(normed, router_weight, routes):
    logits = jnp.dot(
        normed, router_weight, precision=lax.Precision.HIGHEST, preferred_element_type=jnp.float32
    )
    affinity = jax.nn.sigmoid(logits)
    labels = jnp.arange(affinity.shape[1], dtype=jnp.int32)
    picked = jnp.sum(
        jnp.where(
            routes[:, :, None] == labels[None, None, :], affinity[:, None, :], jnp.float32(0.0)
        ),
        axis=-1,
    )
    return route_scale * picked / jnp.sum(picked, axis=1, keepdims=True)


def routed(
    residual, head_partials, norm_gain, router_weight, routes, expert_gate, expert_up, expert_down
):
    tensor_count = lax.axis_size("tensor")
    expert_count = lax.axis_size("expert")
    row_count = residual.shape[0]
    top_count = routes.shape[1]
    capacity = max(2, min(row_count, 3 * row_count * top_count // (2 * expert_count)))
    attention = lax.psum_scatter(
        head_partials[0].astype(jnp.float32).astype(jnp.bfloat16),
        "tensor",
        scatter_dimension=0,
        tiled=True,
    ).astype(jnp.float32)
    stream, normed = prepare(residual, attention, norm_gain)
    payload, scales = quantize(normed, QBLOCK)
    weights = route_weights(normed, router_weight, routes)
    pair_count = row_count * top_count
    flat_routes = routes.reshape(pair_count)
    onehot = (flat_routes[:, None] == jnp.arange(expert_count, dtype=jnp.int32)[None, :]).astype(
        jnp.bfloat16
    )
    pair_index = jnp.arange(pair_count, dtype=jnp.int32)
    lower = (pair_index[:, None] > pair_index[None, :]).astype(jnp.bfloat16)
    ahead = jnp.dot(lower, onehot, preferred_element_type=jnp.float32)
    position = jnp.sum(ahead * onehot.astype(jnp.float32), axis=1).astype(jnp.int32)
    slot = flat_routes * capacity + position
    slot_index = jnp.arange(expert_count * capacity, dtype=jnp.int32)
    place = (slot_index[:, None] == slot[None, :]).astype(jnp.bfloat16)
    place_rows = jnp.sum(place.reshape(expert_count * capacity, row_count, top_count), axis=2)
    send_payload = jnp.dot(place_rows, payload, preferred_element_type=jnp.float32).astype(
        jnp.bfloat16
    )
    send_payload = send_payload.reshape(expert_count, capacity, -1)
    send_scales = jnp.dot(place_rows, scales, preferred_element_type=jnp.float32).astype(
        jnp.bfloat16
    )
    send_scales = send_scales.reshape(expert_count, capacity, -1)
    doubled_payload = jnp.repeat(send_payload, tensor_count, axis=0)
    doubled_scales = jnp.repeat(send_scales, tensor_count, axis=0)
    arriving = lax.all_to_all(
        doubled_payload, ("expert", "tensor"), split_axis=0, concat_axis=0, tiled=True
    )
    arriving_scales = lax.all_to_all(
        doubled_scales, ("expert", "tensor"), split_axis=0, concat_axis=0, tiled=True
    )
    sources = arriving.shape[0]
    slots = arriving.shape[1]
    inputs = dequantize(
        arriving.reshape(sources * slots, -1), arriving_scales.reshape(sources * slots, -1)
    )
    gate_part = jnp.dot(inputs, expert_gate[0], preferred_element_type=jnp.float32)
    up_part = jnp.dot(inputs, expert_up[0], preferred_element_type=jnp.float32)
    activated = (jax.nn.silu(gate_part) * up_part).astype(jnp.bfloat16)
    partial_value = jnp.dot(activated, expert_down[0], preferred_element_type=jnp.float32).astype(
        jnp.bfloat16
    )
    partial_value = partial_value.reshape(sources, slots, -1)
    back = lax.all_to_all(
        partial_value, ("expert", "tensor"), split_axis=0, concat_axis=0, tiled=True
    )
    paired = back.reshape(expert_count, tensor_count, back.shape[1], back.shape[2])
    returned = jnp.sum(paired.astype(jnp.float32), axis=1).astype(jnp.bfloat16)
    flat_return = returned.reshape(expert_count * capacity, -1)
    pair_out = jnp.dot(place.T, flat_return, preferred_element_type=jnp.float32)
    moe_sum = jnp.sum(pair_out.reshape(row_count, top_count, -1) * weights[:, :, None], axis=1)
    return (stream.astype(jnp.float32) + moe_sum).astype(jnp.bfloat16)


LAYERS = 4


def pick(table, z):
    value = table[0]
    for i in range(1, LAYERS):
        value = value + (table[i] - table[i - 1]) * ((z + LAYERS - i) // LAYERS)
    return value


def local_rows(
    residual_ref, heads_ref, gain_ref, router_ref, routes_ref,
    stream_ref, normed_ref, spread_ref, rows, mine,
):
    n, width = residual_ref.shape
    experts = router_ref.shape[0]
    top_count = routes_ref.shape[1]

    def block_cols(i):
        return pl.ds(pl.multiple_of(i * QBLOCK, QBLOCK), QBLOCK)

    def add_attention(i, squares):
        cols = block_cols(i)
        value = residual_ref[:, cols].astype(jnp.float32) + heads_ref[:, cols].astype(jnp.float32)
        value = value.astype(jnp.bfloat16)
        stream_ref[:, cols] = value
        value = value.astype(jnp.float32)
        return squares + value * value

    squares = lax.fori_loop(
        0, width // QBLOCK, add_attention, jnp.zeros((n, QBLOCK), jnp.float32), unroll=4
    )
    factor = lax.rsqrt(jnp.sum(squares, axis=1, keepdims=True) * (1.0 / width) + epsilon)

    def scale_block(i, carry):
        cols = block_cols(i)
        normed = stream_ref[:, cols].astype(jnp.float32) * factor * gain_ref[:, cols]
        normed_ref[:, cols] = normed
        scale = (jnp.max(jnp.abs(normed), axis=1, keepdims=True) + epsilon) / scale_limit
        scale = scale.astype(jnp.bfloat16).astype(jnp.float32)
        payload = (normed / scale).astype(jnp.bfloat16).astype(jnp.float32)
        rows[mine, cols] = (payload * scale).astype(jnp.bfloat16)
        return carry

    lax.fori_loop(0, width // QBLOCK, scale_block, 0, unroll=4)

    logits = lax.dot_general(
        normed_ref[...], router_ref[...], (((1,), (1,)), ((), ())),
        precision=lax.Precision.HIGHEST, preferred_element_type=jnp.float32,
    )
    affinity = 1.0 / (1.0 + jnp.exp(-logits))
    labels = lax.broadcasted_iota(jnp.int32, (n, experts), 1)
    picked = jnp.zeros((n, experts), jnp.float32)
    for k in range(top_count):
        picked = picked + jnp.where(routes_ref[:, k : k + 1] == labels, affinity, 0.0)
    weights = route_scale * picked / jnp.sum(picked, axis=1, keepdims=True)
    spread_ref[...] = jnp.zeros_like(spread_ref)
    for piece in range(3):
        top = weights.astype(jnp.bfloat16).astype(jnp.float32)
        spread_ref[:, piece * experts : (piece + 1) * experts] = top
        weights = weights - top
    rows[mine, width:] = spread_ref[...].astype(jnp.bfloat16)


def layer_kernel(
    residual_ref, heads_ref, gain_ref, router_ref, routes_ref, gate_hbm, up_hbm, down_hbm, out_ref,
    stream_ref, normed_ref, spread_ref,
    rows, parts, from_core, from_x, from_z, hidden, gate, up, down,
    send_up, send_dn, send_x, send_core, got_rows,
    back_core, back_x, back_z, got_core, got_x, got_z, weight_sem,
):
    n, width = stream_ref.shape
    full = rows.shape[1]
    inner = hidden.shape[1]
    experts = LAYERS * 4
    me = lax.axis_index("expert")
    z, x, c = me // 4, (me // 2) % 2, me % 2
    core_dev = me + 1 - 2 * c
    x_dev = me + 2 - 4 * x
    up_dev, dn_dev = me + 4, me - 4

    def block(layer, xx, cc):
        return layer * 4 + xx * 2 + cc

    def span(b):
        return pl.ds(pl.multiple_of(b * n, n), n)

    barrier = pltpu.get_barrier_semaphore()

    def greet(dev):
        pl.semaphore_signal(
            barrier, inc=1, device_id={"expert": dev}, device_id_type=pl.DeviceIdType.MESH
        )

    greet(core_dev)
    greet(x_dev)
    pl.when(z > 0)(lambda: greet(dn_dev))
    pl.when(z < LAYERS - 1)(lambda: greet(up_dev))

    loads = [
        pltpu.make_async_copy(src.at[0], dst, weight_sem.at[i])
        for i, (src, dst) in enumerate(((gate_hbm, gate), (up_hbm, up), (down_hbm, down)))
    ]
    for load in loads:
        load.start()
    local_rows(
        residual_ref, heads_ref, gain_ref, router_ref, routes_ref,
        stream_ref, normed_ref, spread_ref, rows, span(me),
    )
    pl.semaphore_wait(barrier, 2 + (z + LAYERS - 1) // LAYERS + (2 * LAYERS - 2 - z) // LAYERS)

    def remote(src, dst, ssem, rsem, dev):
        return pltpu.make_async_remote_copy(
            src_ref=src, dst_ref=dst, send_sem=ssem, recv_sem=rsem,
            device_id={"expert": dev}, device_id_type=pl.DeviceIdType.MESH,
        )

    def row_copy(b, sems, dev):
        return remote(rows.at[span(b)], rows.at[span(b)], sems.at[b], got_rows.at[b], dev)

    def arrived(b):
        row_copy(b, send_core, core_dev).wait_recv()

    row_copy(me, send_x, x_dev).start()
    pl.when(z > 0)(lambda: row_copy(me, send_dn, dn_dev).start())
    pl.when(z < LAYERS - 1)(lambda: row_copy(me, send_up, up_dev).start())
    row_copy(me, send_core, core_dev).start()

    def from_line(layer, sems, onward, dev):
        b = block(layer, x, c)
        arrived(b)
        pl.when(onward)(lambda: row_copy(b, sems, dev).start())
        row_copy(b, send_x, x_dev).start()
        row_copy(b, send_core, core_dev).start()

    def line_step(s):
        pl.when(z >= s)(lambda: from_line(z - s, send_up, z < LAYERS - 1, up_dev))
        pl.when(z + s < LAYERS)(lambda: from_line(z + s, send_dn, z > 0, dn_dev))

    def rest_of(layer):
        b = block(layer, 1 - x, c)
        arrived(b)
        row_copy(b, send_core, core_dev).start()
        arrived(block(layer, 0, 1 - c))
        arrived(block(layer, 1, 1 - c))

    def layer_span(layer):
        return pl.ds(pl.multiple_of(layer * 4 * n, 4 * n), 4 * n)

    half = (width // 512 + 1) // 2 * 512
    chunks = ((0, half), (half, width - half))

    def part(h):
        return pl.ds(chunks[h][0], chunks[h][1])

    def gate_up(layer):
        where = layer_span(layer)

        @pl.loop(0, inner // 256)
        def _(i):
            cols = pl.ds(pl.multiple_of(i * 256, 256), 256)
            inputs = rows[where, :width]
            g = jnp.dot(inputs, gate[:, cols], preferred_element_type=jnp.float32)
            u = jnp.dot(inputs, up[:, cols], preferred_element_type=jnp.float32)
            hidden[:, cols] = (g / (1.0 + jnp.exp(-g)) * u).astype(jnp.bfloat16)

    def down_back(layer):
        where = layer_span(layer)
        lane = lax.broadcasted_iota(jnp.int32, (4 * n, full - width), 1)
        mine = (lane == me) | (lane == me + experts) | (lane == me + 2 * experts)
        factor = jnp.sum(
            jnp.where(mine, rows[where, width:].astype(jnp.float32), 0.0), axis=1, keepdims=True
        )
        for h in range(2):

            @pl.loop(chunks[h][0] // 512, sum(chunks[h]) // 512)
            def _(i):
                cols = pl.ds(pl.multiple_of(i * 512, 512), 512)
                o = jnp.dot(hidden[...], down[:, cols], preferred_element_type=jnp.float32)
                parts[where, cols] = (o * factor).astype(jnp.bfloat16)

            for xx in (1 - x, x):
                core_back(layer, xx, 1 - c, h).start()

    def core_back(layer, xx, cc, h):
        slot = layer * 2 + xx
        return remote(
            parts.at[span(block(layer, xx, cc)), part(h)], from_core.at[slot, :, part(h)],
            back_core.at[slot, h], got_core.at[slot, h], core_dev,
        )

    def x_back(layer, h):
        return remote(
            parts.at[span(block(layer, 1 - x, c)), part(h)], from_x.at[layer, :, part(h)],
            back_x.at[layer, h], got_x.at[layer, h], x_dev,
        )

    def z_back(layer, slot, dev, h):
        return remote(
            parts.at[span(block(layer, x, c)), part(h)], from_z.at[slot, :, part(h)],
            back_z.at[layer, h], got_z.at[slot, h], dev,
        )

    def add_up(dst, dst_rows, terms, h):
        @pl.loop(chunks[h][0] // 512, sum(chunks[h]) // 512)
        def _(i):
            cols = pl.ds(pl.multiple_of(i * 512, 512), 512)
            total = None
            for ref, where in terms:
                term = ref[where, cols].astype(jnp.float32)
                total = term if total is None else total + term
            dst[dst_rows, cols] = total.astype(jnp.bfloat16)

    whole = slice(None)

    def ret_x(layer):
        b = span(block(layer, 1 - x, c))
        for h in range(2):
            core_back(layer, 1 - x, c, h).wait_recv()
            add_up(parts, b, [(parts, b), (from_core.at[layer * 2 + 1 - x], whole)], h)
            x_back(layer, h).start()

    def ret_z(layer):
        b = span(block(layer, x, c))
        terms = [
            (parts, b), (from_core.at[layer * 2 + x], whole), (from_x.at[layer], whole),
        ]
        carries = ((layer > z) & (z > 0)) | ((layer < z) & (z < LAYERS - 1))
        for h in range(2):
            core_back(layer, x, c, h).wait_recv()
            x_back(layer, h).wait_recv()

            @pl.when(carries)
            def _():
                z_back(layer, layer, up_dev, h).wait_recv()
                add_up(parts, b, terms + [(from_z.at[layer], whole)], h)

            @pl.when(jnp.logical_not(carries))
            def _():
                add_up(parts, b, terms, h)

            @pl.when(layer > z)
            def _():
                z_back(layer, layer, up_dev, h).start()

            @pl.when((layer < z) & (layer < z - 1))
            def _():
                z_back(layer, layer, dn_dev, h).start()

            @pl.when((layer < z) & (layer == z - 1))
            def _():
                z_back(layer, LAYERS, dn_dev, h).start()

    order = [
        z,
        pick((1, 2, 1, 2), z),
        pick((2, 0, 3, 1), z),
        pick((3, 3, 0, 0), z),
    ]
    back_order = [order[1], pick((2, 3, 0, 1), z), pick((3, 0, 3, 0), z)]
    ends = (z == 0) | (z == LAYERS - 1)

    line_step(1)
    rest_of(order[0])
    loads[0].wait()
    loads[1].wait()
    gate_up(order[0])
    loads[2].wait()
    down_back(order[0])
    line_step(2)
    rest_of(order[1])
    gate_up(order[1])
    down_back(order[1])
    line_step(3)
    rest_of(order[2])
    gate_up(order[2])
    ret_x(order[1])
    down_back(order[2])
    rest_of(order[3])
    gate_up(order[3])
    ret_x(order[2])
    pl.when(ends)(lambda: ret_z(order[1]))
    down_back(order[3])
    ret_x(order[3])
    pl.when(ends)(lambda: ret_z(order[2]))
    ret_x(order[0])
    pl.when(ends)(lambda: ret_z(order[3]))

    @pl.when(jnp.logical_not(ends))
    def _():
        for layer in back_order:
            ret_z(layer)

    b = span(me)
    terms = [
        (stream_ref, whole), (parts, b), (from_core.at[z * 2 + x], whole), (from_x.at[z], whole),
    ]
    below, above = (from_z.at[z], whole), (from_z.at[LAYERS], whole)
    for h in range(2):
        core_back(z, x, c, h).wait_recv()
        x_back(z, h).wait_recv()

        @pl.when(z > 0)
        def _():
            z_back(z, z, up_dev, h).wait_recv()

        @pl.when(z < LAYERS - 1)
        def _():
            z_back(z, LAYERS, up_dev, h).wait_recv()

        @pl.when(z == 0)
        def _():
            add_up(out_ref, whole, terms + [above], h)

        @pl.when(z == LAYERS - 1)
        def _():
            add_up(out_ref, whole, terms + [below], h)

        @pl.when((z > 0) & (z < LAYERS - 1))
        def _():
            add_up(out_ref, whole, terms + [below, above], h)

    for layer in range(LAYERS):
        mine = block(layer, x, c)
        row_copy(mine, send_x, x_dev).wait_send()
        row_copy(mine, send_core, core_dev).wait_send()
        row_copy(block(layer, 1 - x, c), send_core, core_dev).wait_send()

        @pl.when((layer <= z) & (z < LAYERS - 1))
        def _():
            row_copy(mine, send_up, up_dev).wait_send()

        @pl.when((layer >= z) & (z > 0))
        def _():
            row_copy(mine, send_dn, dn_dev).wait_send()

        for h in range(2):
            for xx in range(2):
                core_back(layer, xx, 1 - c, h).wait_send()
            x_back(layer, h).wait_send()

            @pl.when(z != layer)
            def _():
                z_back(layer, layer, up_dev, h).wait_send()


def dense(
    residual, head_partials, norm_gain, router_weight, routes, expert_gate, expert_up, expert_down
):
    n, width = residual.shape
    full = width + 128
    inner = expert_gate.shape[2]
    total = 4 * LAYERS
    dma = pltpu.SemaphoreType.DMA
    bf16 = jnp.bfloat16
    return pl.pallas_call(
        layer_kernel,
        out_shape=jax.ShapeDtypeStruct((n, width), bf16),
        in_specs=[pl.BlockSpec(memory_space=pltpu.VMEM)] * 5
        + [pl.BlockSpec(memory_space=pl.ANY)] * 3,
        out_specs=pl.BlockSpec(memory_space=pltpu.VMEM),
        scratch_shapes=[
            pltpu.VMEM((n, width), bf16),
            pltpu.VMEM((n, width), jnp.float32),
            pltpu.VMEM((n, 128), jnp.float32),
            pltpu.VMEM((total * n, full), bf16),
            pltpu.VMEM((total * n, width), bf16),
            pltpu.VMEM((2 * LAYERS, n, width), bf16),
            pltpu.VMEM((LAYERS, n, width), bf16),
            pltpu.VMEM((LAYERS + 1, n, width), bf16),
            pltpu.VMEM((4 * n, inner), bf16),
            pltpu.VMEM((width, inner), bf16),
            pltpu.VMEM((width, inner), bf16),
            pltpu.VMEM((inner, width), bf16),
            dma((total,)), dma((total,)), dma((total,)), dma((total,)), dma((total,)),
            dma((2 * LAYERS, 2)), dma((LAYERS, 2)), dma((LAYERS, 2)),
            dma((2 * LAYERS, 2)), dma((LAYERS, 2)), dma((LAYERS + 1, 2)),
            dma((3,)),
        ],
        compiler_params=pltpu.CompilerParams(
            collective_id=0, has_side_effects=True, vmem_limit_bytes=60 * 1024 * 1024
        ),
    )(
        residual, head_partials[0], norm_gain[None], router_weight.T, routes,
        expert_gate, expert_up, expert_down,
    )


def local(*args):
    if lax.axis_size("tensor") == 1 and lax.axis_size("expert") == 4 * LAYERS:
        return dense(*args)
    return routed(*args)


def solution(mesh):
    return jax.shard_map(
        local,
        mesh=mesh,
        in_specs=(
            P(("group", "expert", "tensor"), None),
            P("tensor", ("group", "expert"), None),
            P(),
            P(),
            P(("group", "expert", "tensor"), None),
            P("expert", None, "tensor"),
            P("expert", None, "tensor"),
            P("expert", "tensor", None),
        ),
        out_specs=P(("group", "expert", "tensor"), None),
        check_vma=False,
    )
```

```python
import jax
import jax.numpy as jnp
from jax import lax
from jax.experimental import pallas as pl
from jax.experimental.pallas import tpu as pltpu
from jax.sharding import PartitionSpec as P

QBLOCK = 128


epsilon = 1e-06
scale_limit = 448.0
route_scale = 2.5


def prepare(residual, attention, norm_gain):
    stream = (residual.astype(jnp.float32) + attention).astype(jnp.bfloat16)
    values = stream.astype(jnp.float32)
    normed = (
        values * lax.rsqrt(jnp.mean(values * values, axis=-1, keepdims=True) + epsilon) * norm_gain
    )
    return (stream, normed)


def quantize(normed, block_size):
    row_count = normed.shape[0]
    blocks = normed.reshape(row_count, -1, block_size)
    scales = ((jnp.max(jnp.abs(blocks), axis=-1) + epsilon) / scale_limit).astype(jnp.bfloat16)
    payload = (blocks / scales.astype(jnp.float32)[:, :, None]).astype(jnp.bfloat16)
    return (payload.reshape(row_count, -1), scales)


def dequantize(payload, scales):
    row_count = payload.shape[0]
    block_size = payload.shape[1] // scales.shape[1]
    blocks = payload.astype(jnp.float32).reshape(row_count, scales.shape[1], block_size)
    blocks = blocks * scales.astype(jnp.float32)[:, :, None]
    return blocks.reshape(row_count, -1).astype(jnp.bfloat16)


def route_weights(normed, router_weight, routes):
    logits = jnp.dot(
        normed, router_weight, precision=lax.Precision.HIGHEST, preferred_element_type=jnp.float32
    )
    affinity = jax.nn.sigmoid(logits)
    labels = jnp.arange(affinity.shape[1], dtype=jnp.int32)
    picked = jnp.sum(
        jnp.where(
            routes[:, :, None] == labels[None, None, :], affinity[:, None, :], jnp.float32(0.0)
        ),
        axis=-1,
    )
    return route_scale * picked / jnp.sum(picked, axis=1, keepdims=True)


def routed(
    residual, head_partials, norm_gain, router_weight, routes, expert_gate, expert_up, expert_down
):
    tensor_count = lax.axis_size("tensor")
    expert_count = lax.axis_size("expert")
    row_count = residual.shape[0]
    top_count = routes.shape[1]
    capacity = max(2, min(row_count, 3 * row_count * top_count // (2 * expert_count)))
    attention = lax.psum_scatter(
        head_partials[0].astype(jnp.float32).astype(jnp.bfloat16),
        "tensor",
        scatter_dimension=0,
        tiled=True,
    ).astype(jnp.float32)
    stream, normed = prepare(residual, attention, norm_gain)
    payload, scales = quantize(normed, QBLOCK)
    weights = route_weights(normed, router_weight, routes)
    pair_count = row_count * top_count
    flat_routes = routes.reshape(pair_count)
    onehot = (flat_routes[:, None] == jnp.arange(expert_count, dtype=jnp.int32)[None, :]).astype(
        jnp.bfloat16
    )
    pair_index = jnp.arange(pair_count, dtype=jnp.int32)
    lower = (pair_index[:, None] > pair_index[None, :]).astype(jnp.bfloat16)
    ahead = jnp.dot(lower, onehot, preferred_element_type=jnp.float32)
    position = jnp.sum(ahead * onehot.astype(jnp.float32), axis=1).astype(jnp.int32)
    slot = flat_routes * capacity + position
    slot_index = jnp.arange(expert_count * capacity, dtype=jnp.int32)
    place = (slot_index[:, None] == slot[None, :]).astype(jnp.bfloat16)
    place_rows = jnp.sum(place.reshape(expert_count * capacity, row_count, top_count), axis=2)
    send_payload = jnp.dot(place_rows, payload, preferred_element_type=jnp.float32).astype(
        jnp.bfloat16
    )
    send_payload = send_payload.reshape(expert_count, capacity, -1)
    send_scales = jnp.dot(place_rows, scales, preferred_element_type=jnp.float32).astype(
        jnp.bfloat16
    )
    send_scales = send_scales.reshape(expert_count, capacity, -1)
    doubled_payload = jnp.repeat(send_payload, tensor_count, axis=0)
    doubled_scales = jnp.repeat(send_scales, tensor_count, axis=0)
    arriving = lax.all_to_all(
        doubled_payload, ("expert", "tensor"), split_axis=0, concat_axis=0, tiled=True
    )
    arriving_scales = lax.all_to_all(
        doubled_scales, ("expert", "tensor"), split_axis=0, concat_axis=0, tiled=True
    )
    sources = arriving.shape[0]
    slots = arriving.shape[1]
    inputs = dequantize(
        arriving.reshape(sources * slots, -1), arriving_scales.reshape(sources * slots, -1)
    )
    gate_part = jnp.dot(inputs, expert_gate[0], preferred_element_type=jnp.float32)
    up_part = jnp.dot(inputs, expert_up[0], preferred_element_type=jnp.float32)
    activated = (jax.nn.silu(gate_part) * up_part).astype(jnp.bfloat16)
    partial_value = jnp.dot(activated, expert_down[0], preferred_element_type=jnp.float32).astype(
        jnp.bfloat16
    )
    partial_value = partial_value.reshape(sources, slots, -1)
    back = lax.all_to_all(
        partial_value, ("expert", "tensor"), split_axis=0, concat_axis=0, tiled=True
    )
    paired = back.reshape(expert_count, tensor_count, back.shape[1], back.shape[2])
    returned = jnp.sum(paired.astype(jnp.float32), axis=1).astype(jnp.bfloat16)
    flat_return = returned.reshape(expert_count * capacity, -1)
    pair_out = jnp.dot(place.T, flat_return, preferred_element_type=jnp.float32)
    moe_sum = jnp.sum(pair_out.reshape(row_count, top_count, -1) * weights[:, :, None], axis=1)
    return (stream.astype(jnp.float32) + moe_sum).astype(jnp.bfloat16)


LAYERS = 4


def pick(table, z):
    value = table[0]
    for i in range(1, LAYERS):
        value = value + (table[i] - table[i - 1]) * ((z + LAYERS - i) // LAYERS)
    return value


def local_rows(
    residual_ref, heads_ref, gain_ref, router_ref, routes_ref,
    stream_ref, normed_ref, spread_ref, rows, mine,
):
    n, width = residual_ref.shape
    experts = router_ref.shape[0]
    top_count = routes_ref.shape[0]

    def block_cols(i):
        return pl.ds(pl.multiple_of(i * QBLOCK, QBLOCK), QBLOCK)

    def add_attention(i, squares):
        cols = block_cols(i)
        value = residual_ref[:, cols].astype(jnp.float32) + heads_ref[:, cols].astype(jnp.float32)
        value = value.astype(jnp.bfloat16)
        stream_ref[:, cols] = value
        value = value.astype(jnp.float32)
        return squares + value * value

    squares = lax.fori_loop(
        0, width // QBLOCK, add_attention, jnp.zeros((n, QBLOCK), jnp.float32), unroll=4
    )
    factor = lax.rsqrt(jnp.sum(squares, axis=1, keepdims=True) * (1.0 / width) + epsilon)

    def scale_block(i, carry):
        cols = block_cols(i)
        normed = stream_ref[:, cols].astype(jnp.float32) * factor * gain_ref[pl.ds(i, 1), :]
        normed_ref[:, cols] = normed
        scale = (jnp.max(jnp.abs(normed), axis=1, keepdims=True) + epsilon) / scale_limit
        scale = scale.astype(jnp.bfloat16).astype(jnp.float32)
        payload = (normed / scale).astype(jnp.bfloat16).astype(jnp.float32)
        rows[mine, cols] = (payload * scale).astype(jnp.bfloat16)
        return carry

    lax.fori_loop(0, width // QBLOCK, scale_block, 0, unroll=4)

    logits = lax.dot_general(
        normed_ref[...], router_ref[...], (((1,), (1,)), ((), ())),
        precision=lax.Precision.HIGHEST, preferred_element_type=jnp.float32,
    )
    affinity = 1.0 / (1.0 + jnp.exp(-logits))
    labels = lax.broadcasted_iota(jnp.int32, (experts, n), 0)
    member = jnp.zeros((experts, n), jnp.float32)
    for k in range(top_count):
        member = member + jnp.where(routes_ref[k : k + 1, :] == labels, 1.0, 0.0)
    unit = lax.broadcasted_iota(jnp.int32, (experts, experts), 0)
    unit = unit == lax.broadcasted_iota(jnp.int32, (experts, experts), 1)
    member = lax.dot_general(
        member, jnp.where(unit, 1.0, 0.0), (((0,), (0,)), ((), ())),
        preferred_element_type=jnp.float32,
    )
    picked = jnp.where(member > 0.5, affinity, 0.0)
    weights = route_scale * picked / jnp.sum(picked, axis=1, keepdims=True)
    spread_ref[...] = jnp.zeros_like(spread_ref)
    for piece in range(3):
        top = weights.astype(jnp.bfloat16).astype(jnp.float32)
        spread_ref[:, piece * experts : (piece + 1) * experts] = top
        weights = weights - top
    rows[mine, width:] = spread_ref[...].astype(jnp.bfloat16)


def layer_kernel(
    residual_ref, heads_ref, gain_ref, router_ref, routes_ref, gate_hbm, up_hbm, down_hbm, out_ref,
    stream_ref, normed_ref, spread_ref,
    rows, parts, from_core, from_x, from_z, hidden, gate, up, down,
    send_up, send_dn, send_x, send_core, got_rows,
    back_core, back_x, back_z, got_core, got_x, got_z, weight_sem,
):
    n, width = stream_ref.shape
    full = rows.shape[1]
    inner = hidden.shape[1]
    experts = LAYERS * 4
    me = lax.axis_index("expert")
    z, x, c = me // 4, (me // 2) % 2, me % 2
    core_dev = me + 1 - 2 * c
    x_dev = me + 2 - 4 * x
    up_dev, dn_dev = me + 4, me - 4

    def block(layer, xx, cc):
        return layer * 4 + xx * 2 + cc

    def span(b):
        return pl.ds(pl.multiple_of(b * n, n), n)

    barrier = pltpu.get_barrier_semaphore()

    def greet(dev):
        pl.semaphore_signal(
            barrier, inc=1, device_id={"expert": dev}, device_id_type=pl.DeviceIdType.MESH
        )

    greet(core_dev)
    greet(x_dev)
    pl.when(z > 0)(lambda: greet(dn_dev))
    pl.when(z < LAYERS - 1)(lambda: greet(up_dev))

    loads = [
        pltpu.make_async_copy(src.at[0], dst, weight_sem.at[i])
        for i, (src, dst) in enumerate(((gate_hbm, gate), (up_hbm, up), (down_hbm, down)))
    ]
    for load in loads:
        load.start()
    local_rows(
        residual_ref, heads_ref, gain_ref, router_ref, routes_ref,
        stream_ref, normed_ref, spread_ref, rows, span(me),
    )
    pl.semaphore_wait(barrier, 2 + (z + LAYERS - 1) // LAYERS + (2 * LAYERS - 2 - z) // LAYERS)

    def remote(src, dst, ssem, rsem, dev):
        return pltpu.make_async_remote_copy(
            src_ref=src, dst_ref=dst, send_sem=ssem, recv_sem=rsem,
            device_id={"expert": dev}, device_id_type=pl.DeviceIdType.MESH,
        )

    def row_copy(b, sems, dev):
        return remote(rows.at[span(b)], rows.at[span(b)], sems.at[b], got_rows.at[b], dev)

    def arrived(b):
        row_copy(b, send_core, core_dev).wait_recv()

    row_copy(me, send_x, x_dev).start()
    pl.when(z > 0)(lambda: row_copy(me, send_dn, dn_dev).start())
    pl.when(z < LAYERS - 1)(lambda: row_copy(me, send_up, up_dev).start())
    row_copy(me, send_core, core_dev).start()

    def from_line(layer, sems, onward, dev):
        b = block(layer, x, c)
        arrived(b)
        pl.when(onward)(lambda: row_copy(b, sems, dev).start())
        row_copy(b, send_x, x_dev).start()
        row_copy(b, send_core, core_dev).start()

    def line_step(s):
        pl.when(z >= s)(lambda: from_line(z - s, send_up, z < LAYERS - 1, up_dev))
        pl.when(z + s < LAYERS)(lambda: from_line(z + s, send_dn, z > 0, dn_dev))

    def rest_of(layer):
        b = block(layer, 1 - x, c)
        arrived(b)
        row_copy(b, send_core, core_dev).start()
        arrived(block(layer, 0, 1 - c))
        arrived(block(layer, 1, 1 - c))

    def layer_span(layer):
        return pl.ds(pl.multiple_of(layer * 4 * n, 4 * n), 4 * n)

    half = (width // 512 + 1) // 2 * 512
    chunks = ((0, half), (half, width - half))

    def part(h):
        return pl.ds(chunks[h][0], chunks[h][1])

    def gate_up(layer):
        where = layer_span(layer)

        @pl.loop(0, inner // 256)
        def _(i):
            cols = pl.ds(pl.multiple_of(i * 256, 256), 256)
            inputs = rows[where, :width]
            g = jnp.dot(inputs, gate[:, cols], preferred_element_type=jnp.float32)
            u = jnp.dot(inputs, up[:, cols], preferred_element_type=jnp.float32)
            hidden[:, cols] = (g / (1.0 + jnp.exp(-g)) * u).astype(jnp.bfloat16)

    def down_back(layer):
        where = layer_span(layer)
        lane = lax.broadcasted_iota(jnp.int32, (4 * n, full - width), 1)
        mine = (lane == me) | (lane == me + experts) | (lane == me + 2 * experts)
        factor = jnp.sum(
            jnp.where(mine, rows[where, width:].astype(jnp.float32), 0.0), axis=1, keepdims=True
        )
        for h in range(2):

            @pl.loop(chunks[h][0] // 512, sum(chunks[h]) // 512)
            def _(i):
                cols = pl.ds(pl.multiple_of(i * 512, 512), 512)
                o = jnp.dot(hidden[...], down[:, cols], preferred_element_type=jnp.float32)
                parts[where, cols] = (o * factor).astype(jnp.bfloat16)

            for xx in (1 - x, x):
                core_back(layer, xx, 1 - c, h).start()

    def core_back(layer, xx, cc, h):
        slot = layer * 2 + xx
        return remote(
            parts.at[span(block(layer, xx, cc)), part(h)], from_core.at[slot, :, part(h)],
            back_core.at[slot, h], got_core.at[slot, h], core_dev,
        )

    def x_back(layer, h):
        return remote(
            parts.at[span(block(layer, 1 - x, c)), part(h)], from_x.at[layer, :, part(h)],
            back_x.at[layer, h], got_x.at[layer, h], x_dev,
        )

    def z_back(layer, slot, dev, h):
        return remote(
            parts.at[span(block(layer, x, c)), part(h)], from_z.at[slot, :, part(h)],
            back_z.at[layer, h], got_z.at[slot, h], dev,
        )

    def add_up(dst, dst_rows, terms, h):
        @pl.loop(chunks[h][0] // 512, sum(chunks[h]) // 512)
        def _(i):
            cols = pl.ds(pl.multiple_of(i * 512, 512), 512)
            total = None
            for ref, where in terms:
                term = ref[where, cols].astype(jnp.float32)
                total = term if total is None else total + term
            dst[dst_rows, cols] = total.astype(jnp.bfloat16)

    whole = slice(None)

    def ret_x(layer):
        b = span(block(layer, 1 - x, c))
        for h in range(2):
            core_back(layer, 1 - x, c, h).wait_recv()
            add_up(parts, b, [(parts, b), (from_core.at[layer * 2 + 1 - x], whole)], h)
            x_back(layer, h).start()

    def ret_z(layer):
        b = span(block(layer, x, c))
        terms = [
            (parts, b), (from_core.at[layer * 2 + x], whole), (from_x.at[layer], whole),
        ]
        carries = ((layer > z) & (z > 0)) | ((layer < z) & (z < LAYERS - 1))
        for h in range(2):
            core_back(layer, x, c, h).wait_recv()
            x_back(layer, h).wait_recv()

            @pl.when(carries)
            def _():
                z_back(layer, layer, up_dev, h).wait_recv()
                add_up(parts, b, terms + [(from_z.at[layer], whole)], h)

            @pl.when(jnp.logical_not(carries))
            def _():
                add_up(parts, b, terms, h)

            @pl.when(layer > z)
            def _():
                z_back(layer, layer, up_dev, h).start()

            @pl.when((layer < z) & (layer < z - 1))
            def _():
                z_back(layer, layer, dn_dev, h).start()

            @pl.when((layer < z) & (layer == z - 1))
            def _():
                z_back(layer, LAYERS, dn_dev, h).start()

    order = [
        z,
        pick((1, 2, 1, 2), z),
        pick((2, 0, 3, 1), z),
        pick((3, 3, 0, 0), z),
    ]
    back_order = [order[1], pick((2, 3, 0, 1), z), pick((3, 0, 3, 0), z)]
    ends = (z == 0) | (z == LAYERS - 1)

    line_step(1)
    rest_of(order[0])
    loads[0].wait()
    loads[1].wait()
    gate_up(order[0])
    loads[2].wait()
    down_back(order[0])
    line_step(2)
    rest_of(order[1])
    gate_up(order[1])
    down_back(order[1])
    line_step(3)
    rest_of(order[2])
    gate_up(order[2])
    ret_x(order[1])
    down_back(order[2])
    rest_of(order[3])
    gate_up(order[3])
    ret_x(order[2])
    pl.when(ends)(lambda: ret_z(order[1]))
    down_back(order[3])
    ret_x(order[3])
    pl.when(ends)(lambda: ret_z(order[2]))
    ret_x(order[0])
    pl.when(ends)(lambda: ret_z(order[3]))

    @pl.when(jnp.logical_not(ends))
    def _():
        for layer in back_order:
            ret_z(layer)

    b = span(me)
    terms = [
        (stream_ref, whole), (parts, b), (from_core.at[z * 2 + x], whole), (from_x.at[z], whole),
    ]
    below, above = (from_z.at[z], whole), (from_z.at[LAYERS], whole)
    for h in range(2):
        core_back(z, x, c, h).wait_recv()
        x_back(z, h).wait_recv()

        @pl.when(z > 0)
        def _():
            z_back(z, z, up_dev, h).wait_recv()

        @pl.when(z < LAYERS - 1)
        def _():
            z_back(z, LAYERS, up_dev, h).wait_recv()

        @pl.when(z == 0)
        def _():
            add_up(out_ref, whole, terms + [above], h)

        @pl.when(z == LAYERS - 1)
        def _():
            add_up(out_ref, whole, terms + [below], h)

        @pl.when((z > 0) & (z < LAYERS - 1))
        def _():
            add_up(out_ref, whole, terms + [below, above], h)

    for layer in range(LAYERS):
        mine = block(layer, x, c)
        row_copy(mine, send_x, x_dev).wait_send()
        row_copy(mine, send_core, core_dev).wait_send()
        row_copy(block(layer, 1 - x, c), send_core, core_dev).wait_send()

        @pl.when((layer <= z) & (z < LAYERS - 1))
        def _():
            row_copy(mine, send_up, up_dev).wait_send()

        @pl.when((layer >= z) & (z > 0))
        def _():
            row_copy(mine, send_dn, dn_dev).wait_send()

        for h in range(2):
            for xx in range(2):
                core_back(layer, xx, 1 - c, h).wait_send()
            x_back(layer, h).wait_send()

            @pl.when(z != layer)
            def _():
                z_back(layer, layer, up_dev, h).wait_send()


def dense(
    residual, head_partials, norm_gain, router_weight, routes, expert_gate, expert_up, expert_down
):
    n, width = residual.shape
    full = width + 128
    inner = expert_gate.shape[2]
    total = 4 * LAYERS
    dma = pltpu.SemaphoreType.DMA
    bf16 = jnp.bfloat16
    return pl.pallas_call(
        layer_kernel,
        out_shape=jax.ShapeDtypeStruct((n, width), bf16),
        in_specs=[pl.BlockSpec(memory_space=pltpu.VMEM)] * 5
        + [pl.BlockSpec(memory_space=pl.ANY)] * 3,
        out_specs=pl.BlockSpec(memory_space=pltpu.VMEM),
        scratch_shapes=[
            pltpu.VMEM((n, width), bf16),
            pltpu.VMEM((n, width), jnp.float32),
            pltpu.VMEM((n, 128), jnp.float32),
            pltpu.VMEM((total * n, full), bf16),
            pltpu.VMEM((total * n, width), bf16),
            pltpu.VMEM((2 * LAYERS, n, width), bf16),
            pltpu.VMEM((LAYERS, n, width), bf16),
            pltpu.VMEM((LAYERS + 1, n, width), bf16),
            pltpu.VMEM((4 * n, inner), bf16),
            pltpu.VMEM((width, inner), bf16),
            pltpu.VMEM((width, inner), bf16),
            pltpu.VMEM((inner, width), bf16),
            dma((total,)), dma((total,)), dma((total,)), dma((total,)), dma((total,)),
            dma((2 * LAYERS, 2)), dma((LAYERS, 2)), dma((LAYERS, 2)),
            dma((2 * LAYERS, 2)), dma((LAYERS, 2)), dma((LAYERS + 1, 2)),
            dma((3,)),
        ],
        compiler_params=pltpu.CompilerParams(
            collective_id=0, has_side_effects=True, vmem_limit_bytes=60 * 1024 * 1024
        ),
    )(
        residual, head_partials[0], norm_gain.reshape(-1, QBLOCK), router_weight.T, routes.T,
        expert_gate, expert_up, expert_down,
    )


def local(*args):
    if lax.axis_size("tensor") == 1 and lax.axis_size("expert") == 4 * LAYERS:
        return dense(*args)
    return routed(*args)


def solution(mesh):
    return jax.shard_map(
        local,
        mesh=mesh,
        in_specs=(
            P(("group", "expert", "tensor"), None),
            P("tensor", ("group", "expert"), None),
            P(),
            P(),
            P(("group", "expert", "tensor"), None),
            P("expert", None, "tensor"),
            P("expert", None, "tensor"),
            P("expert", "tensor", None),
        ),
        out_specs=P(("group", "expert", "tensor"), None),
        check_vma=False,
    )
```
